32 devices in a mesh: grp: 2 (over x), row: 16 (over z, y, core).
Axes of the slice: x: 2, y: 2, z: 4, core: 2. Of those that a mesh axis runs over, the one named last changes fastest.
Arguments:
- cell_coeffs: float32 [6, 32, 384], P(None, 'row'), may hold values from 0.5 to 2
- z_factor: float32 [4, 64, 384, 128], P(None, ('grp', 'row')), parts along dimension 1, may hold values from -0.022552745 to 0.022552745
- noise_cols: float32 [4, 64, 384, 128], P(None, ('grp', 'row')), parts along dimension 1, may hold values from -0.022552745 to 0.022552745
- q_bar: float32 [4, 64, 384, 256], P(None, ('grp', 'row')), parts along dimension 1, may hold values from -10 to 10
- r_bar: float32 [512, 256], P('grp'), parts along dimension 0, may hold values from -11.085125 to 11.085125
Outputs:
- z_grad: float32 [4, 64, 384, 128], P(None, ('grp', 'row')), parts along dimension 1
- noise_grad: float32 [4, 64, 384, 128], P(None, ('grp', 'row')), parts along dimension 1
The draws below stay inside these ranges and needn't reach their ends.
There are 2 independent parts, one for each index of `grp`. The reference program is written for one: setup_inputs(seed, part) draws one part's arguments, and reference() takes and returns one part's arrays. A program takes and returns all parts, laid end to end along the dimension named above; an argument that names none is the same for every part. Nothing has to cross between parts.
All inputs are finite; a program needn't handle non-finite values.
Results may differ from the reference program's by a relative error of at most 0.000061.
Values sent between devices are 32-bit elements; how exact they have to be, the bound alone decides.
A program may use at most 64 MiB of HBM per device.

```python
import math
import jax
import jax.numpy as jnp
from jax import lax

LX = 384
K = 128
KN = 128
NR = 32
ROWS = 49152


def draw_piece(key, shape):
    return jnp.clip(jax.random.normal(key, shape, jnp.float32), -5.0, 5.0)


def draw_shared(key):
    spread = float(ROWS) ** (-0.5)
    base_z = draw_piece(jax.random.fold_in(key, 11), (4, NR, LX, K))
    base_n = draw_piece(jax.random.fold_in(key, 12), (4, NR, LX, KN))
    loose = draw_piece(jax.random.fold_in(key, 13), (4, NR, LX, K + KN))
    bar_q = jnp.concatenate([base_z, base_n], axis=3) + loose
    bar_r = jnp.clip(jax.random.normal(jax.random.fold_in(key, 14), (K + KN, K + KN), jnp.float32), -5.0, 5.0) * (0.01 * float(ROWS) ** 0.5)
    return (base_z * spread, base_n * spread, bar_q, bar_r)


def draw_z_factor(key, part):
    return draw_shared(key)[0]


def draw_noise_cols(key, part):
    return draw_shared(key)[1]


def draw_q_bar(key, part):
    return draw_shared(key)[2]


def draw_r_bar(key, part):
    return draw_shared(key)[3]


def levels(key, shape, split, least, high):
    loudness = 1.0
    for position, blocks in split:
        draws = jax.random.uniform(jax.random.fold_in(jax.random.fold_in(key, 6), position), (blocks,), jnp.float32, least / len(split), high / len(split))
        loudness = loudness * jnp.repeat(jnp.exp(draws), shape[position] // blocks).reshape((-1,) + (1,) * (len(shape) - 1 - position))
    return loudness


def setup_inputs(seed: int = 0, part: int = 0) -> dict:
    key_of = jax.random.split(jax.random.key(seed), 6)
    part_splits = jax.random.split(jax.random.fold_in(key_of[5], part), 6)
    return {
        "cell_coeffs": jnp.clip(jnp.exp(math.log(2.0) - 1.3862944 * jax.random.uniform(key_of[0], (6, NR, LX), jnp.float32) ** levels(key_of[0], (6, NR, LX), ((1, 16),), -0.2, 0.2)), 0.5, 2.0),
        "z_factor": draw_z_factor(jax.random.fold_in(jax.random.fold_in(key_of[5], part), 71), part),
        "noise_cols": draw_noise_cols(jax.random.fold_in(jax.random.fold_in(key_of[5], part), 71), part),
        "q_bar": draw_q_bar(jax.random.fold_in(jax.random.fold_in(key_of[5], part), 71), part),
        "r_bar": draw_r_bar(jax.random.fold_in(jax.random.fold_in(key_of[5], part), 71), part),
    }


rate_scales = (0.4, 0.4, 0.1, 0.2, 0.1, 0.1)
exact = lax.Precision.HIGHEST

def local_part(values, scaled, transposed):
    detuning = scaled[0][..., None]
    mech_freq = scaled[1][..., None]
    coupling = scaled[2][..., None]
    cavity_loss = scaled[3][..., None]
    phonon_loss = scaled[4][..., None]
    light_x, light_p, motion_x, motion_p = (values[0], values[1], values[2], values[3])
    if transposed:
        return jnp.stack([-0.5 * cavity_loss * light_x + detuning * light_p - 2.0 * coupling * motion_p, -detuning * light_x - 0.5 * cavity_loss * light_p, -2.0 * coupling * light_p - mech_freq * motion_p, mech_freq * motion_x - 0.5 * phonon_loss * motion_p])
    return jnp.stack([-0.5 * cavity_loss * light_x - detuning * light_p, detuning * light_x - 0.5 * cavity_loss * light_p - 2.0 * coupling * motion_x, mech_freq * motion_p, -mech_freq * motion_x - 0.5 * phonon_loss * motion_p - 2.0 * coupling * light_x])

def hop_sources(values, scaled, transposed):
    hopping = scaled[5][..., None]
    if transposed:
        return jnp.stack([hopping * values[0], hopping * values[1]])
    return jnp.stack([values[1], values[0]])

def neighbours(source):
    middle = source[:, 1:-1]
    sideways = jnp.pad(middle, ((0, 0), (0, 0), (1, 1), (0, 0)))
    return source[:, :-2] + source[:, 2:] + sideways[:, :, :-2] + sideways[:, :, 2:]

def hop_add(local_term, hop_sums, scaled, transposed):
    hopping = scaled[5][..., None]
    if transposed:
        return jnp.stack([local_term[0] + hop_sums[1], local_term[1] - hop_sums[0], local_term[2], local_term[3]])
    return jnp.stack([local_term[0] - hopping * hop_sums[0], local_term[1] + hopping * hop_sums[1], local_term[2], local_term[3]])

def apply_full(values, scaled, transposed):
    source = hop_sources(values, scaled, transposed)
    extended = jnp.pad(source, ((0, 0), (1, 1), (0, 0), (0, 0)))
    return hop_add(local_part(values, scaled, transposed), neighbours(extended), scaled, transposed)

def expand(values, scaled, transposed):
    first_term = apply_full(values, scaled, transposed)
    second = apply_full(first_term, scaled, transposed)
    return values + first_term + 0.5 * second

def reference(cell_coeffs, z_factor, noise_cols, q_bar, r_bar):
    scaled = cell_coeffs * jnp.array(rate_scales, jnp.float32)[:, None, None]
    rank_cols = z_factor.shape[3]
    stacked = jnp.concatenate([expand(z_factor, scaled, False), noise_cols], axis=3)
    flat_rows = stacked.reshape(-1, stacked.shape[3])
    bar_rows = q_bar.reshape(-1, q_bar.shape[3])
    gram_matrix = jnp.einsum('ik,il->kl', flat_rows, flat_rows, precision=exact)
    lower_factor = jnp.linalg.cholesky(gram_matrix)
    identity = jnp.eye(gram_matrix.shape[0], dtype=jnp.float32)
    r_inv = lax.linalg.triangular_solve(lower_factor, identity, left_side=True, lower=True).T
    upper_factor = lower_factor.T
    q_fact = jnp.dot(flat_rows, r_inv, precision=exact)
    cross = jnp.einsum('ik,il->kl', bar_rows, q_fact, precision=exact)
    middle = jnp.dot(upper_factor, jnp.triu(r_bar).T, precision=exact) - cross
    symmetric = jnp.tril(middle) + jnp.tril(middle, -1).T
    grad_rows = jnp.dot(bar_rows + jnp.dot(q_fact, symmetric, precision=exact), r_inv.T, precision=exact)
    grad_x = grad_rows.reshape(q_bar.shape)
    z_grad = expand(grad_x[..., :rank_cols], scaled, True)
    return (z_grad, grad_x[..., rank_cols:])
```

```python
import functools

import jax
import jax.numpy as jnp
from jax import lax
from jax.experimental import pallas as pl
from jax.experimental.pallas import tpu as pltpu
from jax.sharding import PartitionSpec as P

rate_scales = (0.4, 0.4, 0.1, 0.2, 0.1, 0.1)
extra_scales = (1.0, 1.0, 2.0, 0.5, 0.5, 1.0)
exact = lax.Precision.HIGHEST

parts = 6
margin = 8
lag = 2
tile = 32


def reduction(count, part_ref, half_in, half_sum, quarter_in, quarter_sum, piece_in, full, send_sem, recv_sem, peer_send, peer_recv, back_send, back_recv):
    rows = part_ref.shape[0]
    peers = count // 4
    half, quarter, piece = rows // 2, rows // 4, rows // count
    me = lax.axis_index("row")
    low, mid, top = lax.rem(me, 2), lax.rem(me // 2, 2), me // 4
    pair = me + 1 - 2 * low
    across = me + 2 - 4 * mid

    def other(step):
        return lax.rem(top + step, peers)

    def copy_to(source, target, sends, recvs, slot, where):
        return pltpu.make_async_remote_copy(
            src_ref=source,
            dst_ref=target,
            send_sem=sends.at[slot],
            recv_sem=recvs.at[slot],
            device_id={"row": where},
            device_id_type=pl.DeviceIdType.MESH,
        )

    first = copy_to(
        part_ref.at[pl.ds(pl.multiple_of((1 - low) * half, 8), half)], half_in, send_sem, recv_sem, 0, pair
    )
    first.start()
    yield
    first.wait()
    half_sum[...] = part_ref[pl.ds(pl.multiple_of(low * half, 8), half)] + half_in[...]
    second = copy_to(
        half_sum.at[pl.ds(pl.multiple_of((1 - mid) * quarter, 8), quarter)], quarter_in, send_sem, recv_sem, 1, across
    )
    second.start()
    yield
    second.wait()
    quarter_sum[...] = half_sum[pl.ds(pl.multiple_of(mid * quarter, 8), quarter)] + quarter_in[...]
    outgoing = [
        copy_to(
            quarter_sum.at[pl.ds(pl.multiple_of(other(step) * piece, 8), piece)],
            piece_in.at[step],
            peer_send,
            peer_recv,
            step,
            other(step) * 4 + lax.rem(me, 4),
        )
        for step in range(1, peers)
    ]
    for copy in outgoing:
        copy.start()
    yield
    total = quarter_sum[pl.ds(pl.multiple_of(top * piece, 8), piece)]
    for step, copy in enumerate(outgoing, 1):
        copy.wait()
        total = total + piece_in[step]
    base = low * half + mid * quarter
    mine = pl.ds(pl.multiple_of(base + top * piece, 8), piece)
    full[mine] = total
    returning = [
        copy_to(full.at[mine], full.at[mine], back_send, back_recv, step, other(step) * 4 + lax.rem(me, 4))
        for step in range(1, peers)
    ]
    for copy in returning:
        copy.start()
    yield
    for copy in returning:
        copy.wait()
    own_quarter = full.at[pl.ds(pl.multiple_of(base, 8), quarter)]
    third = copy_to(own_quarter, own_quarter, send_sem, recv_sem, 2, across)
    third.start()
    yield
    third.wait()
    own_half = full.at[pl.ds(pl.multiple_of(low * half, 8), half)]
    fourth = copy_to(own_half, own_half, send_sem, recv_sem, 3, pair)
    fourth.start()
    yield
    fourth.wait()


def reduction_scratch(count, rows, cols):
    peers = count // 4
    return [
        pltpu.VMEM((rows, cols), jnp.float32),
        pltpu.VMEM((rows // 2, cols), jnp.float32),
        pltpu.VMEM((rows // 2, cols), jnp.float32),
        pltpu.VMEM((rows // 4, cols), jnp.float32),
        pltpu.VMEM((rows // 4, cols), jnp.float32),
        pltpu.VMEM((peers, rows // count, cols), jnp.float32),
        pltpu.VMEM((rows, cols), jnp.float32),
        pltpu.SemaphoreType.DMA((4,)),
        pltpu.SemaphoreType.DMA((4,)),
    ] + [pltpu.SemaphoreType.DMA((peers,))] * 4


def tile_inverse(block):
    shape = (tile, tile)
    row_ids = lax.broadcasted_iota(jnp.int32, shape, 0)
    col_ids = lax.broadcasted_iota(jnp.int32, shape, 1)
    right = (row_ids == col_ids).astype(jnp.float32)
    left = block
    scale = jnp.zeros(shape, jnp.float32)
    for start in range(0, tile, 8):
        columns = [
            jnp.broadcast_to(left[start:, start + k : start + k + 1], (tile - start, tile)) for k in range(8)
        ]
        below_left, below_right = left[start:], right[start:]
        ids = row_ids[start:]
        for j in range(8):
            pivot = columns[j][j : j + 1]
            factor = jnp.where(ids > start + j, columns[j] * (1.0 / pivot), 0.0)
            scale = jnp.where(row_ids == start + j, lax.rsqrt(pivot), scale)
            for k in range(j + 1, 8):
                columns[k] = columns[k] - factor * columns[k][j : j + 1]
            below_left = below_left - factor * below_left[j : j + 1]
            below_right = below_right - factor * below_right[j : j + 1]
        if start:
            left = jnp.concatenate([left[:start], below_left], axis=0)
            right = jnp.concatenate([right[:start], below_right], axis=0)
        else:
            left, right = below_left, below_right
    return right * scale


def mul(a, b, contract):
    return lax.dot_general(a, b, ((contract[0:1], contract[1:2]), ((), ())), precision=exact, preferred_element_type=jnp.float32)


def dot16(a, b, contract):
    return lax.dot_general(a, b, ((contract[0:1], contract[1:2]), ((), ())), preferred_element_type=jnp.float32)


def halves(value):
    high = value.astype(jnp.bfloat16)
    return high, (value - high.astype(jnp.float32)).astype(jnp.bfloat16)


def whole_kernel(
    count, coef_ref, z_hbm, noise_hbm, bar_hbm, rbar_ref, z_out, noise_out,
    coef_rows, halo_rows, coefs, values, hop, second, first, partial, light, halo,
    noise_in, bar_in, all_high, all_low, acc_z, acc_n, work, weight_z, weight_n,
    load_sem, send_low, recv_low, send_high, recv_high, *sums,
):
    quads, rows, cells, cols = z_hbm.shape
    size = 2 * cols
    chunk = cells // parts
    strips = quads * rows
    block = strips * chunk
    me = lax.axis_index("row")
    has_low, has_high = me > 0, me < count - 1
    gram_scratch, cross_scratch = sums[:13], sums[13:]
    gram_part, gram_full = gram_scratch[0], gram_scratch[6]
    cross_part, cross_full = cross_scratch[0], cross_scratch[6]

    load_z = pltpu.make_async_copy(z_hbm, values.at[:, :, margin : margin + cells], load_sem.at[0])
    load_noise = pltpu.make_async_copy(noise_hbm, noise_in, load_sem.at[1])
    load_bar = pltpu.make_async_copy(bar_hbm, bar_in, load_sem.at[2])
    load_z.start()

    barrier = pltpu.get_barrier_semaphore()
    peers = count // 4
    low, mid, top = lax.rem(me, 2), lax.rem(me // 2, 2), me // 4
    friends = [me + 1 - 2 * low, me + 2 - 4 * mid]
    friends += [lax.rem(top + step, peers) * 4 + lax.rem(me, 4) for step in range(1, peers)]

    @pl.when(has_low)
    def _():
        pl.semaphore_signal(barrier, inc=1, device_id={"row": me - 1}, device_id_type=pl.DeviceIdType.MESH)

    @pl.when(has_high)
    def _():
        pl.semaphore_signal(barrier, inc=1, device_id={"row": me + 1}, device_id_type=pl.DeviceIdType.MESH)

    for friend in friends:
        pl.semaphore_signal(barrier, inc=1, device_id={"row": friend}, device_id_type=pl.DeviceIdType.MESH)
    load_noise.start()
    load_bar.start()

    def link(source, target, slot, upward):
        sends, recvs = (send_high, recv_high) if upward else (send_low, recv_low)
        return pltpu.make_async_remote_copy(
            src_ref=source,
            dst_ref=target,
            send_sem=sends.at[slot],
            recv_sem=recvs.at[slot],
            device_id={"row": me + 1 if upward else me - 1},
            device_id_type=pl.DeviceIdType.MESH,
        )

    def message(source, padded, run, stage, piece, upward):
        offset = margin if padded else 0
        return link(
            source.at[0:2, rows - 1 if upward else 0, pl.ds(offset + piece * chunk, chunk)],
            halo.at[run, 0 if upward else 1, 2 * stage : 2 * stage + 2, pl.ds(piece * chunk, chunk)],
            (2 * run + stage) * parts + piece,
            upward,
        )

    def rates(upward):
        return link(coef_rows.at[8:16], halo_rows.at[0 if upward else 1], 4 * parts, upward)

    def send(copy_of):
        @pl.when(has_high)
        def _():
            copy_of(True).start()

        @pl.when(has_low)
        def _():
            copy_of(False).start()

    def receive(copy_of):
        @pl.when(has_low)
        def _():
            copy_of(True).wait_recv()

        @pl.when(has_high)
        def _():
            copy_of(False).wait_recv()

    def sent(copy_of):
        @pl.when(has_high)
        def _():
            copy_of(True).wait_send()

        @pl.when(has_low)
        def _():
            copy_of(False).wait_send()

    def at(piece):
        return slice(piece * chunk, (piece + 1) * chunk)

    def inner(piece, shift=0):
        return slice(margin + piece * chunk + shift, margin + (piece + 1) * chunk + shift)

    def coef(kind, row, piece):
        return coefs[kind * rows + row, at(piece)]

    def strip(piece, quad, row):
        start = piece * block + (quad * rows + row) * chunk
        return slice(start, start + chunk)

    for kind in range(6):
        for row in range(rows):
            line = coef_ref[kind, row : row + 1] * jnp.float32(rate_scales[kind])
            coef_rows[kind * rows + row : kind * rows + row + 1] = line * jnp.float32(extra_scales[kind])
    coef_rows[12:16] = jnp.zeros((4, cells), jnp.float32)
    columns = coef_rows[...].T
    for index in range(6 * rows):
        coefs[index] = jnp.broadcast_to(columns[:, index : index + 1], (cells, cols))
    for buffer in (values, hop, second):
        for quad in range(2):
            for row in range(rows):
                buffer[quad, row, :margin] = jnp.zeros((margin, cols), jnp.float32)
                buffer[quad, row, margin + cells :] = jnp.zeros((margin, cols), jnp.float32)
    for side, has in enumerate((has_low, has_high)):

        @pl.when(jnp.logical_not(has))
        def _():
            halo[:, side] = jnp.zeros(halo.shape[:1] + halo.shape[2:], jnp.float32)
            halo_rows[side] = jnp.zeros(halo_rows.shape[1:], jnp.float32)

    def local(get, buffer, row, piece, transposed):
        xa, pa, xb, pb = [get(quad, row, piece) for quad in range(4)]
        detuning, mech, coupling, cavity, phonon, hopping = [coef(kind, row, piece) for kind in range(6)]
        hops = [
            buffer[quad, row, inner(piece, -1)] + buffer[quad, row, inner(piece, 1)] + buffer[quad, 1 - row, inner(piece)]
            for quad in range(2)
        ]
        if transposed:
            return (
                detuning * pa - cavity * xa - coupling * pb + hops[1],
                -detuning * xa - cavity * pa - hops[0],
                -coupling * pa - mech * pb,
                mech * xb - phonon * pb,
            )
        return (
            -cavity * xa - detuning * pa - hopping * hops[1],
            detuning * xa - cavity * pa - coupling * xb + hopping * hops[0],
            mech * pb,
            -mech * xb - phonon * pb - coupling * xa,
        )

    def value_at(quad, row, piece):
        return values[quad, row, inner(piece)]

    def first_at(quad, row, piece):
        return first[quad, row, at(piece)]

    def first_term(run, source, piece):
        for row in range(rows):
            for quad, value in enumerate(local(value_at, source, row, piece, run == 1)):
                first[quad, row, at(piece)] = value
                if quad < 2:
                    partial[quad, row, at(piece)] = coef(5, row, piece) * value if run else value
        send(functools.partial(message, partial, False, run, 1, piece))

    def first_halo(run, source, piece):
        receive(functools.partial(message, source, True, run, 0, piece))
        for row in range(rows):
            halo_x, halo_p = halo[run, row, 0, at(piece)], halo[run, row, 1, at(piece)]
            hopping = coef(5, row, piece)
            if run:
                new_x, new_p = first_at(0, row, piece) + halo_p, first_at(1, row, piece) - halo_x
            else:
                new_x = first_at(0, row, piece) - hopping * halo_p
                new_p = first_at(1, row, piece) + hopping * halo_x
            first[0, row, at(piece)] = new_x
            first[1, row, at(piece)] = new_p
            second[0, row, inner(piece)] = hopping * new_x if run else new_x
            second[1, row, inner(piece)] = hopping * new_p if run else new_p

    def second_term(run, row, piece):
        found = local(first_at, second, row, piece, run == 1)
        return [value_at(quad, row, piece) + first_at(quad, row, piece) + 0.5 * found[quad] for quad in range(4)]

    def last_halo(run, source, piece):
        receive(functools.partial(message, partial, False, run, 1, piece))
        found = []
        for row in range(rows):
            beyond = coefs[6 * rows + row, at(piece)]
            own_x, own_p = source[0, row, inner(piece)], source[1, row, inner(piece)]
            halo_x, halo_p = halo[run, row, 2, at(piece)], halo[run, row, 3, at(piece)]
            if run:
                add_x, add_p = 0.5 * (halo_p - beyond * own_x), -0.5 * (halo_x + beyond * own_p)
            else:
                hopping = 0.5 * coef(5, row, piece)
                add_x, add_p = -hopping * (halo_p + beyond * own_x), hopping * (halo_x - beyond * own_p)
            found.append((add_x, add_p))
        return found

    pl.semaphore_wait(barrier, jnp.where(me > 0, 1, 0) + jnp.where(me < count - 1, 1, 0) + len(friends))
    send(rates)
    load_z.wait()
    for piece in range(parts):
        send(functools.partial(message, values, True, 0, 0, piece))
    for piece in range(parts):
        first_term(0, values, piece)

    load_noise.wait()
    load_bar.wait()
    for piece in range(parts):
        for quad in range(quads):
            for row in range(rows):
                where = strip(piece, quad, row)
                all_high[where, cols:size], all_low[where, cols:size] = halves(noise_in[quad, row, at(piece)])
                all_high[where, size:], all_low[where, size:] = halves(bar_in[quad, row, at(piece)])

    def accumulate(acc, start, stop, begin, fresh):
        lines = slice(start, stop)
        high = all_high[lines, begin : begin + cols]
        left = jnp.concatenate([high, all_low[lines, begin : begin + cols]], axis=1)
        both = dot16(left, all_high[lines, begin:], (0, 0))
        found = both[:cols] + both[cols:] + dot16(high, all_low[lines, begin:], (0, 0))
        acc[...] = found if fresh else acc[...] + found

    for piece in range(parts):
        accumulate(acc_n, piece * block, (piece + 1) * block, cols, piece == 0)

    receive(rates)
    sides = [halo_rows[0].T, halo_rows[1].T]
    for side in range(2):
        index = 10 - 8 + (rows - 1 if side == 0 else 0)
        coefs[6 * rows + side] = jnp.broadcast_to(sides[side][:, index : index + 1], (cells, cols))

    def finish(piece):
        for row in range(rows):
            found = second_term(0, row, piece)
            for quad in range(2):
                light[quad, row, at(piece)] = found[quad]
            for quad in range(2, 4):
                where = strip(piece, quad, row)
                all_high[where, :cols], all_low[where, :cols] = halves(found[quad])
        accumulate(acc_z, piece * block + block // 2, (piece + 1) * block, 0, piece == 0)

    for piece in range(parts):
        first_halo(0, values, piece)
        if piece:
            finish(piece - 1)
    finish(parts - 1)
    for piece in range(parts):
        for row, added in enumerate(last_halo(0, values, piece)):
            for quad in range(2):
                where = strip(piece, quad, row)
                all_high[where, :cols], all_low[where, :cols] = halves(light[quad, row, at(piece)] + added[quad])
        accumulate(acc_z, piece * block, piece * block + block // 2, 0, False)

    gram_part[:cols] = acc_z[:, :cols]
    gram_part[cols:size] = acc_z[:, cols:size]
    gram_part[size : size + cols] = acc_n[:, :cols]
    if gram_part.shape[0] > size + cols:
        gram_part[size + cols :] = jnp.zeros((gram_part.shape[0] - size - cols, cols), jnp.float32)
    gram_steps = reduction(count, *gram_scratch)
    next(gram_steps)
    for part, (acc, begin) in enumerate(((acc_z, size), (acc_z, size + cols), (acc_n, cols), (acc_n, size))):
        cross_part[part * cols : (part + 1) * cols] = acc[:, begin : begin + cols]
    for piece in range(parts):
        sent(functools.partial(message, values, True, 0, 0, piece))
        sent(functools.partial(message, partial, False, 0, 1, piece))
    sent(rates)
    cross_steps = reduction(count, *cross_scratch)
    for step in range(1, 7):
        next(gram_steps, None)
        if step >= lag:
            next(cross_steps)

    row_ids = lax.broadcasted_iota(jnp.int32, (size, size), 0)
    col_ids = lax.broadcasted_iota(jnp.int32, (size, size), 1)
    work[:cols, :cols] = gram_full[:cols]
    work[:cols, cols:size] = gram_full[cols:size]
    work[cols:, :cols] = jnp.zeros((cols, cols), jnp.float32)
    work[cols:, cols:size] = gram_full[size : size + cols]
    work[:, size:] = (row_ids == col_ids).astype(jnp.float32)
    for start in range(0, size, tile):
        stop = start + tile
        small = tile_inverse(work[start:stop, start:stop])
        panel = mul(small, work[start:stop, :], (1, 0))
        work[start:stop, :] = panel
        if stop < size:
            base, end = stop // 128 * 128, size + (stop + 127) // 128 * 128
            update = mul(panel[:, base:size].T, panel[:, base:end], (1, 0))
            work[stop:, base:end] = work[stop:, base:end] - update[stop - base :]
        next(cross_steps, None)
    upper = jnp.where(row_ids <= col_ids, work[:, :size], 0.0)
    inverse = jnp.where(row_ids >= col_ids, work[:, size:], 0.0)
    bar = jnp.where(row_ids <= col_ids, rbar_ref[...], 0.0)
    cross = jnp.concatenate(
        [
            jnp.concatenate([cross_full[:cols], cross_full[cols:size]], axis=1),
            jnp.concatenate([cross_full[size : size + cols], cross_full[size + cols :]], axis=1),
        ],
        axis=0,
    )
    middle = mul(upper, bar, (1, 1)) - mul(cross.T, inverse, (1, 1))
    symmetric = jnp.where(row_ids >= col_ids, middle, middle.T)
    mix = mul(inverse.T, mul(symmetric, inverse, (1, 0)), (1, 0))
    for begin, value in ((0, mix), (size, inverse)):
        lines = slice(begin, begin + size)
        high, rest = halves(value)
        weight_z[lines, :cols], weight_z[lines, cols:] = high[:, :cols], rest[:, :cols]
        weight_n[lines, :cols], weight_n[lines, cols:] = high[:, cols:], rest[:, cols:]

    def gradient(weight, piece):
        lines = slice(piece * block, (piece + 1) * block)
        both = dot16(all_high[lines], weight[...], (1, 0))
        return both[:, :cols] + both[:, cols:] + dot16(all_low[lines], weight[:, :cols], (1, 0))

    for piece in range(parts):
        grad = gradient(weight_z, piece)
        for quad in range(quads):
            for row in range(rows):
                start = (quad * rows + row) * chunk
                values[quad, row, inner(piece)] = grad[start : start + chunk]
                if quad < 2:
                    hop[quad, row, inner(piece)] = coef(5, row, piece) * grad[start : start + chunk]
        send(functools.partial(message, hop, True, 1, 0, piece))
        if piece:
            first_term(1, hop, piece - 1)
    first_term(1, hop, parts - 1)
    for piece in range(parts):
        grad = gradient(weight_n, piece)
        for quad in range(quads):
            for row in range(rows):
                start = (quad * rows + row) * chunk
                noise_out[quad, row, at(piece)] = grad[start : start + chunk]

    def finish_back(piece):
        for row in range(rows):
            for quad, value in enumerate(second_term(1, row, piece)):
                z_out[quad, row, at(piece)] = value

    for piece in range(parts):
        first_halo(1, hop, piece)
        if piece:
            finish_back(piece - 1)
    finish_back(parts - 1)
    for piece in range(parts):
        for row, added in enumerate(last_halo(1, hop, piece)):
            for quad in range(2):
                z_out[quad, row, at(piece)] = z_out[quad, row, at(piece)] + added[quad]
    for piece in range(parts):
        sent(functools.partial(message, hop, True, 1, 0, piece))
        sent(functools.partial(message, partial, False, 1, 1, piece))


def on_device(cell_coeffs, z_factor, noise_cols, q_bar, r_bar):
    count = lax.axis_size("row")
    quads, rows, cells, cols = z_factor.shape
    size = 2 * cols
    total = quads * rows * cells
    unit = 8 * count
    gram_rows = (size + cols + unit - 1) // unit * unit
    padded = cells + 2 * margin
    plane = (cells, cols)
    here = pl.BlockSpec(memory_space=pltpu.VMEM)
    far = pl.BlockSpec(memory_space=pl.ANY)

    def floats(*shape):
        return pltpu.VMEM(shape, jnp.float32)

    def shorts(*shape):
        return pltpu.VMEM(shape, jnp.bfloat16)

    return pl.pallas_call(
        functools.partial(whole_kernel, count),
        out_shape=(
            jax.ShapeDtypeStruct(z_factor.shape, jnp.float32),
            jax.ShapeDtypeStruct(noise_cols.shape, jnp.float32),
        ),
        in_specs=[here, far, far, far, here],
        out_specs=(here, here),
        scratch_shapes=[
            floats(16, cells),
            floats(2, 8, cells),
            floats(6 * rows + 2, *plane),
            floats(quads, rows, padded, cols),
            floats(2, rows, padded, cols),
            floats(2, rows, padded, cols),
            floats(quads, rows, *plane),
            floats(2, rows, *plane),
            floats(2, rows, *plane),
            floats(2, 2, 4, *plane),
            floats(quads, rows, *plane),
            floats(quads, rows, cells, size),
            shorts(total, 2 * size),
            shorts(total, 2 * size),
            floats(cols, 2 * size),
            floats(cols, 2 * size - cols),
            floats(size, 2 * size),
            shorts(2 * size, size),
            shorts(2 * size, size),
            pltpu.SemaphoreType.DMA((3,)),
        ]
        + [pltpu.SemaphoreType.DMA((4 * parts + 1,))] * 4
        + reduction_scratch(count, gram_rows, cols)
        + reduction_scratch(count, 4 * cols, cols),
        compiler_params=pltpu.CompilerParams(
            collective_id=0, has_side_effects=True, vmem_limit_bytes=48 * 2**20
        ),
    )(cell_coeffs, z_factor, noise_cols, q_bar, r_bar)


def solution(mesh):
    return jax.shard_map(
        on_device,
        mesh=mesh,
        in_specs=(
            P(None, "row", None),
            P(None, ("grp", "row"), None, None),
            P(None, ("grp", "row"), None, None),
            P(None, ("grp", "row"), None, None),
            P("grp", None),
        ),
        out_specs=(P(None, ("grp", "row"), None, None), P(None, ("grp", "row"), None, None)),
        check_vma=False,
    )
```

```python
import functools

import jax
import jax.numpy as jnp
from jax import lax
from jax.experimental import pallas as pl
from jax.experimental.pallas import tpu as pltpu
from jax.sharding import PartitionSpec as P

rate_scales = (0.4, 0.4, 0.1, 0.2, 0.1, 0.1)
extra_scales = (1.0, 1.0, 2.0, 0.5, 0.5, 1.0)
exact = lax.Precision.HIGHEST

parts = 6
margin = 8
tile = 32


def reduction(count, part_ref, half_in, half_sum, piece_in, full, pair_send, pair_recv, peer_send, peer_recv, back_send, back_recv):
    rows = part_ref.shape[0]
    chips = count // 2
    half, piece = rows // 2, rows // count
    me = lax.axis_index("row")
    low, chip = lax.rem(me, 2), me // 2
    pair = me + 1 - 2 * low

    def other(step):
        return lax.rem(chip + step, chips)

    def copy_to(source, target, sends, recvs, slot, where):
        return pltpu.make_async_remote_copy(
            src_ref=source,
            dst_ref=target,
            send_sem=sends.at[slot],
            recv_sem=recvs.at[slot],
            device_id={"row": where},
            device_id_type=pl.DeviceIdType.MESH,
        )

    first = copy_to(
        part_ref.at[pl.ds(pl.multiple_of((1 - low) * half, 8), half)], half_in, pair_send, pair_recv, 0, pair
    )
    first.start()
    yield
    first.wait()
    half_sum[...] = part_ref[pl.ds(pl.multiple_of(low * half, 8), half)] + half_in[...]
    outgoing = [
        copy_to(
            half_sum.at[pl.ds(pl.multiple_of(other(step) * piece, 8), piece)],
            piece_in.at[step],
            peer_send,
            peer_recv,
            step,
            other(step) * 2 + low,
        )
        for step in range(1, chips)
    ]
    for copy in outgoing:
        copy.start()
    yield
    total = half_sum[pl.ds(pl.multiple_of(chip * piece, 8), piece)]
    for step, copy in enumerate(outgoing, 1):
        copy.wait()
        total = total + piece_in[step]
    mine = pl.ds(pl.multiple_of(low * half + chip * piece, 8), piece)
    full[mine] = total
    returning = [
        copy_to(full.at[mine], full.at[mine], back_send, back_recv, step, other(step) * 2 + low)
        for step in range(1, chips)
    ]
    for copy in returning:
        copy.start()
    yield
    for copy in returning:
        copy.wait()
    own_half = full.at[pl.ds(pl.multiple_of(low * half, 8), half)]
    last = copy_to(own_half, own_half, pair_send, pair_recv, 1, pair)
    last.start()
    yield
    last.wait()


def reduction_scratch(count, rows, cols):
    chips = count // 2
    return [
        pltpu.VMEM((rows, cols), jnp.float32),
        pltpu.VMEM((rows // 2, cols), jnp.float32),
        pltpu.VMEM((rows // 2, cols), jnp.float32),
        pltpu.VMEM((chips, rows // count, cols), jnp.float32),
        pltpu.VMEM((rows, cols), jnp.float32),
        pltpu.SemaphoreType.DMA((2,)),
        pltpu.SemaphoreType.DMA((2,)),
    ] + [pltpu.SemaphoreType.DMA((chips,))] * 4


def tile_inverse(block):
    shape = (tile, tile)
    row_ids = lax.broadcasted_iota(jnp.int32, shape, 0)
    col_ids = lax.broadcasted_iota(jnp.int32, shape, 1)
    right = (row_ids == col_ids).astype(jnp.float32)
    left = block
    scale = jnp.zeros(shape, jnp.float32)
    for start in range(0, tile, 8):
        columns = [
            jnp.broadcast_to(left[start:, start + k : start + k + 1], (tile - start, tile)) for k in range(8)
        ]
        below_left, below_right = left[start:], right[start:]
        ids = row_ids[start:]
        for j in range(8):
            pivot = columns[j][j : j + 1]
            factor = jnp.where(ids > start + j, columns[j] * (1.0 / pivot), 0.0)
            scale = jnp.where(row_ids == start + j, lax.rsqrt(pivot), scale)
            for k in range(j + 1, 8):
                columns[k] = columns[k] - factor * columns[k][j : j + 1]
            below_left = below_left - factor * below_left[j : j + 1]
            below_right = below_right - factor * below_right[j : j + 1]
        if start:
            left = jnp.concatenate([left[:start], below_left], axis=0)
            right = jnp.concatenate([right[:start], below_right], axis=0)
        else:
            left, right = below_left, below_right
    return right * scale


def mul(a, b, contract):
    return lax.dot_general(a, b, ((contract[0:1], contract[1:2]), ((), ())), precision=exact, preferred_element_type=jnp.float32)


def dot16(a, b, contract):
    return lax.dot_general(a, b, ((contract[0:1], contract[1:2]), ((), ())), preferred_element_type=jnp.float32)


def halves(value):
    high = value.astype(jnp.bfloat16)
    return high, (value - high.astype(jnp.float32)).astype(jnp.bfloat16)


def whole_kernel(
    count, coef_ref, z_hbm, noise_hbm, bar_hbm, rbar_ref, z_out, noise_out,
    coef_rows, halo_rows, coefs, values, hop, second, first, partial, light, halo,
    noise_in, bar_in, result, all_high, all_low, acc_z, acc_n, work, weight_z, weight_n,
    load_sem, send_low, recv_low, send_high, recv_high, *sums,
):
    quads, rows, cells, cols = z_hbm.shape
    size = 2 * cols
    chunk = cells // parts
    strips = quads * rows
    block = strips * chunk
    me = lax.axis_index("row")
    has_low, has_high = me > 0, me < count - 1
    gram_scratch, cross_scratch = sums[:11], sums[11:]
    gram_part, gram_full = gram_scratch[0], gram_scratch[4]
    cross_part, cross_full = cross_scratch[0], cross_scratch[4]

    load_z = pltpu.make_async_copy(z_hbm, values.at[:, :, margin : margin + cells], load_sem.at[0])
    load_noise = pltpu.make_async_copy(noise_hbm, noise_in, load_sem.at[1])
    load_bar = pltpu.make_async_copy(bar_hbm, bar_in, load_sem.at[2])
    load_z.start()

    barrier = pltpu.get_barrier_semaphore()
    low, chip = lax.rem(me, 2), me // 2
    friends = [me + 1 - 2 * low]
    friends += [lax.rem(chip + step, count // 2) * 2 + low for step in range(1, count // 2)]

    @pl.when(has_low)
    def _():
        pl.semaphore_signal(barrier, inc=1, device_id={"row": me - 1}, device_id_type=pl.DeviceIdType.MESH)

    @pl.when(has_high)
    def _():
        pl.semaphore_signal(barrier, inc=1, device_id={"row": me + 1}, device_id_type=pl.DeviceIdType.MESH)

    for friend in friends:
        pl.semaphore_signal(barrier, inc=1, device_id={"row": friend}, device_id_type=pl.DeviceIdType.MESH)
    load_noise.start()
    load_bar.start()

    def link(source, target, slot, upward):
        sends, recvs = (send_high, recv_high) if upward else (send_low, recv_low)
        return pltpu.make_async_remote_copy(
            src_ref=source,
            dst_ref=target,
            send_sem=sends.at[slot],
            recv_sem=recvs.at[slot],
            device_id={"row": me + 1 if upward else me - 1},
            device_id_type=pl.DeviceIdType.MESH,
        )

    def message(source, padded, run, stage, piece, upward):
        offset = margin if padded else 0
        return link(
            source.at[0:2, rows - 1 if upward else 0, pl.ds(offset + piece * chunk, chunk)],
            halo.at[run, 0 if upward else 1, 2 * stage : 2 * stage + 2, pl.ds(piece * chunk, chunk)],
            (2 * run + stage) * parts + piece,
            upward,
        )

    def rates(upward):
        return link(coef_rows.at[8:16], halo_rows.at[0 if upward else 1], 4 * parts, upward)

    def send(copy_of):
        @pl.when(has_high)
        def _():
            copy_of(True).start()

        @pl.when(has_low)
        def _():
            copy_of(False).start()

    def receive(copy_of):
        @pl.when(has_low)
        def _():
            copy_of(True).wait_recv()

        @pl.when(has_high)
        def _():
            copy_of(False).wait_recv()

    def sent(copy_of):
        @pl.when(has_high)
        def _():
            copy_of(True).wait_send()

        @pl.when(has_low)
        def _():
            copy_of(False).wait_send()

    def at(piece):
        return slice(piece * chunk, (piece + 1) * chunk)

    def inner(piece, shift=0):
        return slice(margin + piece * chunk + shift, margin + (piece + 1) * chunk + shift)

    def coef(kind, row, piece):
        return coefs[kind * rows + row, at(piece)]

    def strip(piece, quad, row):
        start = piece * block + (quad * rows + row) * chunk
        return slice(start, start + chunk)

    for kind in range(6):
        for row in range(rows):
            line = coef_ref[kind, row : row + 1] * jnp.float32(rate_scales[kind])
            coef_rows[kind * rows + row : kind * rows + row + 1] = line * jnp.float32(extra_scales[kind])
    coef_rows[12:16] = jnp.zeros((4, cells), jnp.float32)
    columns = coef_rows[...].T
    for index in range(6 * rows):
        coefs[index] = jnp.broadcast_to(columns[:, index : index + 1], (cells, cols))
    for buffer in (values, hop, second):
        for quad in range(2):
            for row in range(rows):
                buffer[quad, row, :margin] = jnp.zeros((margin, cols), jnp.float32)
                buffer[quad, row, margin + cells :] = jnp.zeros((margin, cols), jnp.float32)
    for side, has in enumerate((has_low, has_high)):

        @pl.when(jnp.logical_not(has))
        def _():
            halo[:, side] = jnp.zeros(halo.shape[:1] + halo.shape[2:], jnp.float32)
            halo_rows[side] = jnp.zeros(halo_rows.shape[1:], jnp.float32)

    def local(get, buffer, row, piece, transposed):
        xa, pa, xb, pb = [get(quad, row, piece) for quad in range(4)]
        detuning, mech, coupling, cavity, phonon, hopping = [coef(kind, row, piece) for kind in range(6)]
        hops = [
            buffer[quad, row, inner(piece, -1)] + buffer[quad, row, inner(piece, 1)] + buffer[quad, 1 - row, inner(piece)]
            for quad in range(2)
        ]
        if transposed:
            return (
                detuning * pa - cavity * xa - coupling * pb + hops[1],
                -detuning * xa - cavity * pa - hops[0],
                -coupling * pa - mech * pb,
                mech * xb - phonon * pb,
            )
        return (
            -cavity * xa - detuning * pa - hopping * hops[1],
            detuning * xa - cavity * pa - coupling * xb + hopping * hops[0],
            mech * pb,
            -mech * xb - phonon * pb - coupling * xa,
        )

    def value_at(quad, row, piece):
        return values[quad, row, inner(piece)]

    def first_at(quad, row, piece):
        return first[quad, row, at(piece)]

    def first_term(run, source, piece):
        for row in range(rows):
            for quad, value in enumerate(local(value_at, source, row, piece, run == 1)):
                first[quad, row, at(piece)] = value
                if quad < 2:
                    partial[quad, row, at(piece)] = coef(5, row, piece) * value if run else value
        send(functools.partial(message, partial, False, run, 1, piece))

    def first_halo(run, source, piece):
        receive(functools.partial(message, source, True, run, 0, piece))
        for row in range(rows):
            halo_x, halo_p = halo[run, row, 0, at(piece)], halo[run, row, 1, at(piece)]
            hopping = coef(5, row, piece)
            if run:
                new_x, new_p = first_at(0, row, piece) + halo_p, first_at(1, row, piece) - halo_x
            else:
                new_x = first_at(0, row, piece) - hopping * halo_p
                new_p = first_at(1, row, piece) + hopping * halo_x
            first[0, row, at(piece)] = new_x
            first[1, row, at(piece)] = new_p
            second[0, row, inner(piece)] = hopping * new_x if run else new_x
            second[1, row, inner(piece)] = hopping * new_p if run else new_p

    def second_term(run, row, piece):
        found = local(first_at, second, row, piece, run == 1)
        return [value_at(quad, row, piece) + first_at(quad, row, piece) + 0.5 * found[quad] for quad in range(4)]

    def last_halo(run, source, piece):
        receive(functools.partial(message, partial, False, run, 1, piece))
        found = []
        for row in range(rows):
            beyond = coefs[6 * rows + row, at(piece)]
            own_x, own_p = source[0, row, inner(piece)], source[1, row, inner(piece)]
            halo_x, halo_p = halo[run, row, 2, at(piece)], halo[run, row, 3, at(piece)]
            if run:
                add_x, add_p = 0.5 * (halo_p - beyond * own_x), -0.5 * (halo_x + beyond * own_p)
            else:
                hopping = 0.5 * coef(5, row, piece)
                add_x, add_p = -hopping * (halo_p + beyond * own_x), hopping * (halo_x - beyond * own_p)
            found.append((add_x, add_p))
        return found

    pl.semaphore_wait(barrier, jnp.where(me > 0, 1, 0) + jnp.where(me < count - 1, 1, 0) + len(friends))
    send(rates)
    load_z.wait()
    for piece in range(parts):
        send(functools.partial(message, values, True, 0, 0, piece))
    for piece in range(parts):
        first_term(0, values, piece)

    load_noise.wait()
    load_bar.wait()
    for piece in range(parts):
        for quad in range(quads):
            for row in range(rows):
                where = strip(piece, quad, row)
                all_high[where, cols:size], all_low[where, cols:size] = halves(noise_in[quad, row, at(piece)])
                all_high[where, size:], all_low[where, size:] = halves(bar_in[quad, row, at(piece)])

    def accumulate(acc, start, stop, begin, fresh):
        lines = slice(start, stop)
        high = all_high[lines, begin : begin + cols]
        left = jnp.concatenate([high, all_low[lines, begin : begin + cols]], axis=1)
        both = dot16(left, all_high[lines, begin:], (0, 0))
        found = both[:cols] + both[cols:] + dot16(high, all_low[lines, begin:], (0, 0))
        acc[...] = found if fresh else acc[...] + found

    for piece in range(parts):
        accumulate(acc_n, piece * block, (piece + 1) * block, cols, piece == 0)

    receive(rates)
    sides = [halo_rows[0].T, halo_rows[1].T]
    for side in range(2):
        index = 10 - 8 + (rows - 1 if side == 0 else 0)
        coefs[6 * rows + side] = jnp.broadcast_to(sides[side][:, index : index + 1], (cells, cols))

    def finish(piece):
        for row in range(rows):
            found = second_term(0, row, piece)
            for quad in range(2):
                light[quad, row, at(piece)] = found[quad]
            for quad in range(2, 4):
                where = strip(piece, quad, row)
                all_high[where, :cols], all_low[where, :cols] = halves(found[quad])
        accumulate(acc_z, piece * block + block // 2, (piece + 1) * block, 0, piece == 0)

    for piece in range(parts):
        first_halo(0, values, piece)
        if piece:
            finish(piece - 1)
    finish(parts - 1)
    for piece in range(parts):
        for row, added in enumerate(last_halo(0, values, piece)):
            for quad in range(2):
                where = strip(piece, quad, row)
                all_high[where, :cols], all_low[where, :cols] = halves(light[quad, row, at(piece)] + added[quad])
        accumulate(acc_z, piece * block, piece * block + block // 2, 0, False)

    gram_part[:cols] = acc_z[:, :cols]
    gram_part[cols:size] = acc_z[:, cols:size]
    gram_part[size : size + cols] = acc_n[:, :cols]
    if gram_part.shape[0] > size + cols:
        gram_part[size + cols :] = jnp.zeros((gram_part.shape[0] - size - cols, cols), jnp.float32)
    gram_steps = reduction(count, *gram_scratch)
    cross_steps = reduction(count, *cross_scratch)
    next(gram_steps)
    for part, (acc, begin) in enumerate(((acc_z, size), (acc_z, size + cols), (acc_n, cols), (acc_n, size))):
        cross_part[part * cols : (part + 1) * cols] = acc[:, begin : begin + cols]
    next(cross_steps)
    next(gram_steps)
    for piece in range(parts):
        sent(functools.partial(message, values, True, 0, 0, piece))
        sent(functools.partial(message, partial, False, 0, 1, piece))
    sent(rates)
    next(gram_steps)
    next(cross_steps)
    next(gram_steps)
    next(gram_steps, None)

    row_ids = lax.broadcasted_iota(jnp.int32, (size, size), 0)
    col_ids = lax.broadcasted_iota(jnp.int32, (size, size), 1)
    work[:cols, :cols] = gram_full[:cols]
    work[:cols, cols:size] = gram_full[cols:size]
    work[cols:, :cols] = jnp.zeros((cols, cols), jnp.float32)
    work[cols:, cols:size] = gram_full[size : size + cols]
    work[:, size:] = (row_ids == col_ids).astype(jnp.float32)
    for start in range(0, size, tile):
        stop = start + tile
        small = tile_inverse(work[start:stop, start:stop])
        panel = mul(small, work[start:stop, :], (1, 0))
        work[start:stop, :] = panel
        if stop < size:
            base, end = stop // 128 * 128, size + (stop + 127) // 128 * 128
            update = mul(panel[:, base:size].T, panel[:, base:end], (1, 0))
            work[stop:, base:end] = work[stop:, base:end] - update[stop - base :]
        if start // tile in (2, 5, 7):
            next(cross_steps, None)
    upper = jnp.where(row_ids <= col_ids, work[:, :size], 0.0)
    inverse = jnp.where(row_ids >= col_ids, work[:, size:], 0.0)
    bar = jnp.where(row_ids <= col_ids, rbar_ref[...], 0.0)
    cross = jnp.concatenate(
        [
            jnp.concatenate([cross_full[:cols], cross_full[cols:size]], axis=1),
            jnp.concatenate([cross_full[size : size + cols], cross_full[size + cols :]], axis=1),
        ],
        axis=0,
    )
    middle = mul(upper, bar, (1, 1)) - mul(cross.T, inverse, (1, 1))
    symmetric = jnp.where(row_ids >= col_ids, middle, middle.T)
    mix = mul(inverse.T, mul(symmetric, inverse, (1, 0)), (1, 0))
    for begin, value in ((0, mix), (size, inverse)):
        lines = slice(begin, begin + size)
        high, rest = halves(value)
        weight_z[lines, :cols], weight_z[lines, cols:] = high[:, :cols], rest[:, :cols]
        weight_n[lines, :cols], weight_n[lines, cols:] = high[:, cols:], rest[:, cols:]

    def gradient(weight, piece):
        lines = slice(piece * block, (piece + 1) * block)
        both = dot16(all_high[lines], weight[...], (1, 0))
        return both[:, :cols] + both[:, cols:] + dot16(all_low[lines], weight[:, :cols], (1, 0))

    for piece in range(parts):
        grad = gradient(weight_z, piece)
        for quad in range(quads):
            for row in range(rows):
                start = (quad * rows + row) * chunk
                values[quad, row, inner(piece)] = grad[start : start + chunk]
                if quad < 2:
                    hop[quad, row, inner(piece)] = coef(5, row, piece) * grad[start : start + chunk]
        send(functools.partial(message, hop, True, 1, 0, piece))
        if piece:
            first_term(1, hop, piece - 1)
    first_term(1, hop, parts - 1)
    for piece in range(parts):
        grad = gradient(weight_n, piece)
        for quad in range(quads):
            for row in range(rows):
                start = (quad * rows + row) * chunk
                noise_in[quad, row, at(piece)] = grad[start : start + chunk]
    store_noise = pltpu.make_async_copy(noise_in, noise_out, load_sem.at[1])
    store_noise.start()

    def finish_back(piece):
        for row in range(rows):
            for quad, value in enumerate(second_term(1, row, piece)):
                result[quad, row, at(piece)] = value

    for piece in range(parts):
        first_halo(1, hop, piece)
        if piece:
            finish_back(piece - 1)
    finish_back(parts - 1)
    stores = [store_noise, pltpu.make_async_copy(result.at[2:4], z_out.at[2:4], load_sem.at[0])]
    stores[1].start()
    for piece in range(parts):
        for row, added in enumerate(last_halo(1, hop, piece)):
            for quad in range(2):
                result[quad, row, at(piece)] = result[quad, row, at(piece)] + added[quad]
        stores.append(pltpu.make_async_copy(result.at[0:2, :, at(piece)], z_out.at[0:2, :, at(piece)], load_sem.at[3 + piece]))
        stores[-1].start()
    for store in stores:
        store.wait()
    for piece in range(parts):
        sent(functools.partial(message, hop, True, 1, 0, piece))
        sent(functools.partial(message, partial, False, 1, 1, piece))


def on_device(cell_coeffs, z_factor, noise_cols, q_bar, r_bar):
    count = lax.axis_size("row")
    quads, rows, cells, cols = z_factor.shape
    size = 2 * cols
    total = quads * rows * cells
    unit = 8 * count
    gram_rows = (size + cols + unit - 1) // unit * unit
    padded = cells + 2 * margin
    plane = (cells, cols)
    here = pl.BlockSpec(memory_space=pltpu.VMEM)
    far = pl.BlockSpec(memory_space=pl.ANY)

    def floats(*shape):
        return pltpu.VMEM(shape, jnp.float32)

    def shorts(*shape):
        return pltpu.VMEM(shape, jnp.bfloat16)

    return pl.pallas_call(
        functools.partial(whole_kernel, count),
        out_shape=(
            jax.ShapeDtypeStruct(z_factor.shape, jnp.float32),
            jax.ShapeDtypeStruct(noise_cols.shape, jnp.float32),
        ),
        in_specs=[here, far, far, far, here],
        out_specs=(far, far),
        scratch_shapes=[
            floats(16, cells),
            floats(2, 8, cells),
            floats(6 * rows + 2, *plane),
            floats(quads, rows, padded, cols),
            floats(2, rows, padded, cols),
            floats(2, rows, padded, cols),
            floats(quads, rows, *plane),
            floats(2, rows, *plane),
            floats(2, rows, *plane),
            floats(2, 2, 4, *plane),
            floats(quads, rows, *plane),
            floats(quads, rows, cells, size),
            floats(quads, rows, *plane),
            shorts(total, 2 * size),
            shorts(total, 2 * size),
            floats(cols, 2 * size),
            floats(cols, 2 * size - cols),
            floats(size, 2 * size),
            shorts(2 * size, size),
            shorts(2 * size, size),
            pltpu.SemaphoreType.DMA((3 + parts,)),
        ]
        + [pltpu.SemaphoreType.DMA((4 * parts + 1,))] * 4
        + reduction_scratch(count, gram_rows, cols)
        + reduction_scratch(count, 4 * cols, cols),
        compiler_params=pltpu.CompilerParams(
            collective_id=0, has_side_effects=True, vmem_limit_bytes=62 * 2**20
        ),
    )(cell_coeffs, z_factor, noise_cols, q_bar, r_bar)


def solution(mesh):
    return jax.shard_map(
        on_device,
        mesh=mesh,
        in_specs=(
            P(None, "row", None),
            P(None, ("grp", "row"), None, None),
            P(None, ("grp", "row"), None, None),
            P(None, ("grp", "row"), None, None),
            P("grp", None),
        ),
        out_specs=(P(None, ("grp", "row"), None, None), P(None, ("grp", "row"), None, None)),
        check_vma=False,
    )
```

```python
import functools

import jax
import jax.numpy as jnp
from jax import lax
from jax.experimental import pallas as pl
from jax.experimental.pallas import tpu as pltpu
from jax.sharding import PartitionSpec as P

rate_scales = (0.4, 0.4, 0.1, 0.2, 0.1, 0.1)
extra_scales = (1.0, 1.0, 2.0, 0.5, 0.5, 1.0)
exact = lax.Precision.HIGHEST

parts = 6
margin = 8
tile = 32


def reduction(count, part_ref, half_in, half_sum, piece_in, full, pair_send, pair_recv, peer_send, peer_recv, back_send, back_recv):
    rows = part_ref.shape[0]
    chips = count // 2
    half, piece = rows // 2, rows // count
    me = lax.axis_index("row")
    low, chip = lax.rem(me, 2), me // 2
    pair = me + 1 - 2 * low

    def other(step):
        return lax.rem(chip + step, chips)

    def copy_to(source, target, sends, recvs, slot, where):
        return pltpu.make_async_remote_copy(
            src_ref=source,
            dst_ref=target,
            send_sem=sends.at[slot],
            recv_sem=recvs.at[slot],
            device_id={"row": where},
            device_id_type=pl.DeviceIdType.MESH,
        )

    first = copy_to(
        part_ref.at[pl.ds(pl.multiple_of((1 - low) * half, 8), half)], half_in, pair_send, pair_recv, 0, pair
    )
    first.start()
    yield
    first.wait()
    half_sum[...] = part_ref[pl.ds(pl.multiple_of(low * half, 8), half)] + half_in[...]
    outgoing = [
        copy_to(
            half_sum.at[pl.ds(pl.multiple_of(other(step) * piece, 8), piece)],
            piece_in.at[step],
            peer_send,
            peer_recv,
            step,
            other(step) * 2 + low,
        )
        for step in range(1, chips)
    ]
    for copy in outgoing:
        copy.start()
    yield
    total = half_sum[pl.ds(pl.multiple_of(chip * piece, 8), piece)]
    for step, copy in enumerate(outgoing, 1):
        copy.wait()
        total = total + piece_in[step]
    mine = pl.ds(pl.multiple_of(low * half + chip * piece, 8), piece)
    full[mine] = total
    returning = [
        copy_to(full.at[mine], full.at[mine], back_send, back_recv, step, other(step) * 2 + low)
        for step in range(1, chips)
    ]
    for copy in returning:
        copy.start()
    yield
    for copy in returning:
        copy.wait()
    own_half = full.at[pl.ds(pl.multiple_of(low * half, 8), half)]
    last = copy_to(own_half, own_half, pair_send, pair_recv, 1, pair)
    last.start()
    yield
    last.wait()


def reduction_scratch(count, rows, cols):
    chips = count // 2
    return [
        pltpu.VMEM((rows, cols), jnp.float32),
        pltpu.VMEM((rows // 2, cols), jnp.float32),
        pltpu.VMEM((rows // 2, cols), jnp.float32),
        pltpu.VMEM((chips, rows // count, cols), jnp.float32),
        pltpu.VMEM((rows, cols), jnp.float32),
        pltpu.SemaphoreType.DMA((2,)),
        pltpu.SemaphoreType.DMA((2,)),
    ] + [pltpu.SemaphoreType.DMA((chips,))] * 4


def tile_inverse(block):
    shape = (tile, tile)
    row_ids = lax.broadcasted_iota(jnp.int32, shape, 0)
    col_ids = lax.broadcasted_iota(jnp.int32, shape, 1)
    right = (row_ids == col_ids).astype(jnp.float32)
    left = block
    scale = jnp.zeros(shape, jnp.float32)
    for start in range(0, tile, 8):
        columns = [
            jnp.broadcast_to(left[start:, start + k : start + k + 1], (tile - start, tile)) for k in range(8)
        ]
        below_left, below_right = left[start:], right[start:]
        ids = row_ids[start:]
        for j in range(8):
            pivot = columns[j][j : j + 1]
            factor = jnp.where(ids > start + j, columns[j] * (1.0 / pivot), 0.0)
            scale = jnp.where(row_ids == start + j, lax.rsqrt(pivot), scale)
            for k in range(j + 1, 8):
                columns[k] = columns[k] - factor * columns[k][j : j + 1]
            below_left = below_left - factor * below_left[j : j + 1]
            below_right = below_right - factor * below_right[j : j + 1]
        if start:
            left = jnp.concatenate([left[:start], below_left], axis=0)
            right = jnp.concatenate([right[:start], below_right], axis=0)
        else:
            left, right = below_left, below_right
    return right * scale


def mul(a, b, contract):
    return lax.dot_general(a, b, ((contract[0:1], contract[1:2]), ((), ())), precision=exact, preferred_element_type=jnp.float32)


def dot16(a, b, contract):
    return lax.dot_general(a, b, ((contract[0:1], contract[1:2]), ((), ())), preferred_element_type=jnp.float32)


def thirds(value):
    high = value.astype(jnp.bfloat16)
    value = value - high.astype(jnp.float32)
    mid = value.astype(jnp.bfloat16)
    return high, mid, (value - mid.astype(jnp.float32)).astype(jnp.bfloat16)


def packed(left, right):
    lh, lm, ll = thirds(left)
    rh, rm, rl = thirds(right)
    return dot16(
        jnp.concatenate([lh, lh, lm, lm, lh, ll], axis=0), jnp.concatenate([rh, rm, rh, rm, rl, rh], axis=0), (0, 0)
    )


def halves(value):
    high = value.astype(jnp.bfloat16)
    return high, (value - high.astype(jnp.float32)).astype(jnp.bfloat16)


def whole_kernel(
    count, coef_hbm, z_hbm, noise_hbm, bar_hbm, rbar_hbm, z_out, noise_out,
    coef_ref, rbar_ref,
    coef_rows, halo_rows, coefs, values, hop, second, first, partial, light, halo,
    noise_in, bar_in, result, all_high, all_low, acc_z, acc_n, work, weight_z, weight_n,
    load_sem, send_low, recv_low, send_high, recv_high, *sums,
):
    quads, rows, cells, cols = z_hbm.shape
    size = 2 * cols
    chunk = cells // parts
    strips = quads * rows
    block = strips * chunk
    me = lax.axis_index("row")
    has_low, has_high = me > 0, me < count - 1
    gram_scratch, cross_scratch = sums[:11], sums[11:]
    gram_part, gram_full = gram_scratch[0], gram_scratch[4]
    cross_part, cross_full = cross_scratch[0], cross_scratch[4]

    load_z = pltpu.make_async_copy(z_hbm, values.at[:, :, margin : margin + cells], load_sem.at[0])
    load_noise = pltpu.make_async_copy(noise_hbm, noise_in, load_sem.at[1])
    load_bar = pltpu.make_async_copy(bar_hbm, bar_in, load_sem.at[2])
    load_coef = pltpu.make_async_copy(coef_hbm, coef_ref, load_sem.at[3])
    load_rbar = pltpu.make_async_copy(rbar_hbm, rbar_ref, load_sem.at[4])
    load_coef.start()
    load_z.start()

    barrier = pltpu.get_barrier_semaphore()
    low, chip = lax.rem(me, 2), me // 2
    friends = [me + 1 - 2 * low]
    friends += [lax.rem(chip + step, count // 2) * 2 + low for step in range(1, count // 2)]

    @pl.when(has_low)
    def _():
        pl.semaphore_signal(barrier, inc=1, device_id={"row": me - 1}, device_id_type=pl.DeviceIdType.MESH)

    @pl.when(has_high)
    def _():
        pl.semaphore_signal(barrier, inc=1, device_id={"row": me + 1}, device_id_type=pl.DeviceIdType.MESH)

    for friend in friends:
        pl.semaphore_signal(barrier, inc=1, device_id={"row": friend}, device_id_type=pl.DeviceIdType.MESH)
    load_noise.start()
    load_bar.start()
    load_rbar.start()

    def link(source, target, slot, upward):
        sends, recvs = (send_high, recv_high) if upward else (send_low, recv_low)
        return pltpu.make_async_remote_copy(
            src_ref=source,
            dst_ref=target,
            send_sem=sends.at[slot],
            recv_sem=recvs.at[slot],
            device_id={"row": me + 1 if upward else me - 1},
            device_id_type=pl.DeviceIdType.MESH,
        )

    def message(source, padded, run, stage, piece, upward):
        offset = margin if padded else 0
        return link(
            source.at[0:2, rows - 1 if upward else 0, pl.ds(offset + piece * chunk, chunk)],
            halo.at[run, 0 if upward else 1, 2 * stage : 2 * stage + 2, pl.ds(piece * chunk, chunk)],
            (2 * run + stage) * parts + piece,
            upward,
        )

    def rates(upward):
        return link(coef_rows.at[8:16], halo_rows.at[0 if upward else 1], 4 * parts, upward)

    def send(copy_of):
        @pl.when(has_high)
        def _():
            copy_of(True).start()

        @pl.when(has_low)
        def _():
            copy_of(False).start()

    def receive(copy_of):
        @pl.when(has_low)
        def _():
            copy_of(True).wait_recv()

        @pl.when(has_high)
        def _():
            copy_of(False).wait_recv()

    def sent(copy_of):
        @pl.when(has_high)
        def _():
            copy_of(True).wait_send()

        @pl.when(has_low)
        def _():
            copy_of(False).wait_send()

    def at(piece):
        return slice(piece * chunk, (piece + 1) * chunk)

    def inner(piece, shift=0):
        return slice(margin + piece * chunk + shift, margin + (piece + 1) * chunk + shift)

    def coef(kind, row, piece):
        return coefs[kind * rows + row, at(piece)]

    def strip(piece, quad, row):
        start = piece * block + (quad * rows + row) * chunk
        return slice(start, start + chunk)

    load_coef.wait()
    for kind in range(6):
        for row in range(rows):
            line = coef_ref[kind, row : row + 1] * jnp.float32(rate_scales[kind])
            coef_rows[kind * rows + row : kind * rows + row + 1] = line * jnp.float32(extra_scales[kind])
    coef_rows[12:16] = jnp.zeros((4, cells), jnp.float32)
    columns = coef_rows[...].T
    for index in range(6 * rows):
        coefs[index] = jnp.broadcast_to(columns[:, index : index + 1], (cells, cols))
    for buffer in (values, hop, second):
        for quad in range(2):
            for row in range(rows):
                buffer[quad, row, :margin] = jnp.zeros((margin, cols), jnp.float32)
                buffer[quad, row, margin + cells :] = jnp.zeros((margin, cols), jnp.float32)
    for side, has in enumerate((has_low, has_high)):

        @pl.when(jnp.logical_not(has))
        def _():
            halo[:, side] = jnp.zeros(halo.shape[:1] + halo.shape[2:], jnp.float32)
            halo_rows[side] = jnp.zeros(halo_rows.shape[1:], jnp.float32)

    def local(get, buffer, row, piece, transposed):
        xa, pa, xb, pb = [get(quad, row, piece) for quad in range(4)]
        detuning, mech, coupling, cavity, phonon, hopping = [coef(kind, row, piece) for kind in range(6)]
        hops = [
            buffer[quad, row, inner(piece, -1)] + buffer[quad, row, inner(piece, 1)] + buffer[quad, 1 - row, inner(piece)]
            for quad in range(2)
        ]
        if transposed:
            return (
                detuning * pa - cavity * xa - coupling * pb + hops[1],
                -detuning * xa - cavity * pa - hops[0],
                -coupling * pa - mech * pb,
                mech * xb - phonon * pb,
            )
        return (
            -cavity * xa - detuning * pa - hopping * hops[1],
            detuning * xa - cavity * pa - coupling * xb + hopping * hops[0],
            mech * pb,
            -mech * xb - phonon * pb - coupling * xa,
        )

    def value_at(quad, row, piece):
        return values[quad, row, inner(piece)]

    def first_at(quad, row, piece):
        return first[quad, row, at(piece)]

    def first_term(run, source, piece):
        for row in range(rows):
            for quad, value in enumerate(local(value_at, source, row, piece, run == 1)):
                first[quad, row, at(piece)] = value
                if quad < 2:
                    partial[quad, row, at(piece)] = coef(5, row, piece) * value if run else value
        send(functools.partial(message, partial, False, run, 1, piece))

    def first_halo(run, source, piece):
        receive(functools.partial(message, source, True, run, 0, piece))
        for row in range(rows):
            halo_x, halo_p = halo[run, row, 0, at(piece)], halo[run, row, 1, at(piece)]
            hopping = coef(5, row, piece)
            if run:
                new_x, new_p = first_at(0, row, piece) + halo_p, first_at(1, row, piece) - halo_x
            else:
                new_x = first_at(0, row, piece) - hopping * halo_p
                new_p = first_at(1, row, piece) + hopping * halo_x
            first[0, row, at(piece)] = new_x
            first[1, row, at(piece)] = new_p
            second[0, row, inner(piece)] = hopping * new_x if run else new_x
            second[1, row, inner(piece)] = hopping * new_p if run else new_p

    def second_term(run, row, piece):
        found = local(first_at, second, row, piece, run == 1)
        return [value_at(quad, row, piece) + first_at(quad, row, piece) + 0.5 * found[quad] for quad in range(4)]

    def last_halo(run, source, piece):
        receive(functools.partial(message, partial, False, run, 1, piece))
        found = []
        for row in range(rows):
            beyond = coefs[6 * rows + row, at(piece)]
            own_x, own_p = source[0, row, inner(piece)], source[1, row, inner(piece)]
            halo_x, halo_p = halo[run, row, 2, at(piece)], halo[run, row, 3, at(piece)]
            if run:
                add_x, add_p = 0.5 * (halo_p - beyond * own_x), -0.5 * (halo_x + beyond * own_p)
            else:
                hopping = 0.5 * coef(5, row, piece)
                add_x, add_p = -hopping * (halo_p + beyond * own_x), hopping * (halo_x - beyond * own_p)
            found.append((add_x, add_p))
        return found

    pl.semaphore_wait(barrier, jnp.where(me > 0, 1, 0) + jnp.where(me < count - 1, 1, 0) + len(friends))
    send(rates)
    load_z.wait()
    for piece in range(parts):
        send(functools.partial(message, values, True, 0, 0, piece))
    for piece in range(parts):
        first_term(0, values, piece)

    load_noise.wait()
    load_bar.wait()
    for piece in range(parts):
        for quad in range(quads):
            for row in range(rows):
                where = strip(piece, quad, row)
                all_high[where, cols:size], all_low[where, cols:size] = halves(noise_in[quad, row, at(piece)])
                all_high[where, size:], all_low[where, size:] = halves(bar_in[quad, row, at(piece)])

    def accumulate(acc, start, stop, begin, fresh):
        lines = slice(start, stop)
        high = all_high[lines, begin : begin + cols]
        left = jnp.concatenate([high, all_low[lines, begin : begin + cols]], axis=1)
        both = dot16(left, all_high[lines, begin:], (0, 0))
        found = both[:cols] + both[cols:] + dot16(high, all_low[lines, begin:], (0, 0))
        acc[...] = found if fresh else acc[...] + found

    for piece in range(parts):
        accumulate(acc_n, piece * block, (piece + 1) * block, cols, piece == 0)

    receive(rates)
    sides = [halo_rows[0].T, halo_rows[1].T]
    for side in range(2):
        index = 10 - 8 + (rows - 1 if side == 0 else 0)
        coefs[6 * rows + side] = jnp.broadcast_to(sides[side][:, index : index + 1], (cells, cols))

    def finish(piece):
        for row in range(rows):
            found = second_term(0, row, piece)
            for quad in range(2):
                light[quad, row, at(piece)] = found[quad]
            for quad in range(2, 4):
                where = strip(piece, quad, row)
                all_high[where, :cols], all_low[where, :cols] = halves(found[quad])
        accumulate(acc_z, piece * block + block // 2, (piece + 1) * block, 0, piece == 0)

    for piece in range(parts):
        first_halo(0, values, piece)
        if piece:
            finish(piece - 1)
    finish(parts - 1)
    for piece in range(parts):
        for row, added in enumerate(last_halo(0, values, piece)):
            for quad in range(2):
                where = strip(piece, quad, row)
                all_high[where, :cols], all_low[where, :cols] = halves(light[quad, row, at(piece)] + added[quad])
        accumulate(acc_z, piece * block, piece * block + block // 2, 0, False)

    gram_part[:cols] = acc_z[:, :cols]
    gram_part[cols:size] = acc_z[:, cols:size]
    gram_part[size : size + cols] = acc_n[:, :cols]
    if gram_part.shape[0] > size + cols:
        gram_part[size + cols :] = jnp.zeros((gram_part.shape[0] - size - cols, cols), jnp.float32)
    gram_steps = reduction(count, *gram_scratch)
    cross_steps = reduction(count, *cross_scratch)
    next(gram_steps)
    for part, (acc, begin) in enumerate(((acc_z, size), (acc_z, size + cols), (acc_n, cols), (acc_n, size))):
        cross_part[part * cols : (part + 1) * cols] = acc[:, begin : begin + cols]
    next(cross_steps)
    next(gram_steps)
    for piece in range(parts):
        sent(functools.partial(message, values, True, 0, 0, piece))
        sent(functools.partial(message, partial, False, 0, 1, piece))
    sent(rates)
    next(gram_steps)
    next(cross_steps)
    next(gram_steps)
    next(cross_steps)
    next(gram_steps, None)

    row_ids = lax.broadcasted_iota(jnp.int32, (size, size), 0)
    col_ids = lax.broadcasted_iota(jnp.int32, (size, size), 1)
    work[:cols, :cols] = gram_full[:cols]
    work[:cols, cols:size] = gram_full[cols:size]
    work[cols:, :cols] = jnp.zeros((cols, cols), jnp.float32)
    work[cols:, cols:size] = gram_full[size : size + cols]
    work[:, size:] = (row_ids == col_ids).astype(jnp.float32)
    for start in range(0, size, tile):
        stop = start + tile
        small = tile_inverse(work[start:stop, start:stop])
        panel = packed(small.T, work[start:stop, :])
        work[start:stop, :] = panel
        if stop < size:
            base, end = stop // 128 * 128, size + (stop + 127) // 128 * 128
            update = packed(panel[:, base:size], panel[:, base:end])
            work[stop:, base:end] = work[stop:, base:end] - update[stop - base :]
        if start // tile in (4, 7):
            next(cross_steps, None)
    upper = jnp.where(row_ids <= col_ids, work[:, :size], 0.0)
    inverse = jnp.where(row_ids >= col_ids, work[:, size:], 0.0)
    load_rbar.wait()
    bar = jnp.where(row_ids <= col_ids, rbar_ref[...], 0.0)
    cross = jnp.concatenate(
        [
            jnp.concatenate([cross_full[:cols], cross_full[cols:size]], axis=1),
            jnp.concatenate([cross_full[size : size + cols], cross_full[size + cols :]], axis=1),
        ],
        axis=0,
    )
    middle = mul(upper, bar, (1, 1)) - mul(cross.T, inverse, (1, 1))
    symmetric = jnp.where(row_ids >= col_ids, middle, middle.T)
    mix = mul(inverse.T, mul(symmetric, inverse, (1, 0)), (1, 0))
    for begin, value in ((0, mix), (size, inverse)):
        lines = slice(begin, begin + size)
        high, rest = halves(value)
        weight_z[lines, :cols], weight_z[lines, cols:] = high[:, :cols], rest[:, :cols]
        weight_n[lines, :cols], weight_n[lines, cols:] = high[:, cols:], rest[:, cols:]

    def gradient(weight, piece):
        lines = slice(piece * block, (piece + 1) * block)
        both = dot16(all_high[lines], weight[...], (1, 0))
        return both[:, :cols] + both[:, cols:] + dot16(all_low[lines], weight[:, :cols], (1, 0))

    for piece in range(parts):
        grad = gradient(weight_z, piece)
        for quad in range(quads):
            for row in range(rows):
                start = (quad * rows + row) * chunk
                values[quad, row, inner(piece)] = grad[start : start + chunk]
                if quad < 2:
                    hop[quad, row, inner(piece)] = coef(5, row, piece) * grad[start : start + chunk]
        send(functools.partial(message, hop, True, 1, 0, piece))
        if piece:
            first_term(1, hop, piece - 1)
    first_term(1, hop, parts - 1)
    for piece in range(parts):
        grad = gradient(weight_n, piece)
        for quad in range(quads):
            for row in range(rows):
                start = (quad * rows + row) * chunk
                noise_in[quad, row, at(piece)] = grad[start : start + chunk]
    store_noise = pltpu.make_async_copy(noise_in, noise_out, load_sem.at[1])
    store_noise.start()

    def finish_back(piece):
        for row in range(rows):
            for quad, value in enumerate(second_term(1, row, piece)):
                result[quad, row, at(piece)] = value

    for piece in range(parts):
        first_halo(1, hop, piece)
        if piece:
            finish_back(piece - 1)
    finish_back(parts - 1)
    stores = [store_noise, pltpu.make_async_copy(result.at[2:4], z_out.at[2:4], load_sem.at[0])]
    stores[1].start()
    for piece in range(parts):
        for row, added in enumerate(last_halo(1, hop, piece)):
            for quad in range(2):
                result[quad, row, at(piece)] = result[quad, row, at(piece)] + added[quad]
        stores.append(pltpu.make_async_copy(result.at[0:2, :, at(piece)], z_out.at[0:2, :, at(piece)], load_sem.at[5 + piece]))
        stores[-1].start()
    for store in stores:
        store.wait()
    for piece in range(parts):
        sent(functools.partial(message, hop, True, 1, 0, piece))
        sent(functools.partial(message, partial, False, 1, 1, piece))


def on_device(cell_coeffs, z_factor, noise_cols, q_bar, r_bar):
    count = lax.axis_size("row")
    quads, rows, cells, cols = z_factor.shape
    size = 2 * cols
    total = quads * rows * cells
    unit = 8 * count
    gram_rows = (size + cols + unit - 1) // unit * unit
    padded = cells + 2 * margin
    plane = (cells, cols)
    far = pl.BlockSpec(memory_space=pl.ANY)

    def floats(*shape):
        return pltpu.VMEM(shape, jnp.float32)

    def shorts(*shape):
        return pltpu.VMEM(shape, jnp.bfloat16)

    return pl.pallas_call(
        functools.partial(whole_kernel, count),
        out_shape=(
            jax.ShapeDtypeStruct(z_factor.shape, jnp.float32),
            jax.ShapeDtypeStruct(noise_cols.shape, jnp.float32),
        ),
        in_specs=[far] * 5,
        out_specs=(far, far),
        scratch_shapes=[
            floats(*cell_coeffs.shape),
            floats(*r_bar.shape),
            floats(16, cells),
            floats(2, 8, cells),
            floats(6 * rows + 2, *plane),
            floats(quads, rows, padded, cols),
            floats(2, rows, padded, cols),
            floats(2, rows, padded, cols),
            floats(quads, rows, *plane),
            floats(2, rows, *plane),
            floats(2, rows, *plane),
            floats(2, 2, 4, *plane),
            floats(quads, rows, *plane),
            floats(quads, rows, cells, size),
            floats(quads, rows, *plane),
            shorts(total, 2 * size),
            shorts(total, 2 * size),
            floats(cols, 2 * size),
            floats(cols, 2 * size - cols),
            floats(size, 2 * size),
            shorts(2 * size, size),
            shorts(2 * size, size),
            pltpu.SemaphoreType.DMA((5 + parts,)),
        ]
        + [pltpu.SemaphoreType.DMA((4 * parts + 1,))] * 4
        + reduction_scratch(count, gram_rows, cols)
        + reduction_scratch(count, 4 * cols, cols),
        compiler_params=pltpu.CompilerParams(
            collective_id=0, has_side_effects=True, vmem_limit_bytes=62 * 2**20
        ),
    )(cell_coeffs, z_factor, noise_cols, q_bar, r_bar)


def solution(mesh):
    return jax.shard_map(
        on_device,
        mesh=mesh,
        in_specs=(
            P(None, "row", None),
            P(None, ("grp", "row"), None, None),
            P(None, ("grp", "row"), None, None),
            P(None, ("grp", "row"), None, None),
            P("grp", None),
        ),
        out_specs=(P(None, ("grp", "row"), None, None), P(None, ("grp", "row"), None, None)),
        check_vma=False,
    )
```

```python
import functools

import jax
import jax.numpy as jnp
from jax import lax
from jax.experimental import pallas as pl
from jax.experimental.pallas import tpu as pltpu
from jax.sharding import PartitionSpec as P

rate_scales = (0.4, 0.4, 0.1, 0.2, 0.1, 0.1)
extra_scales = (1.0, 1.0, 2.0, 0.5, 0.5, 1.0)
exact = lax.Precision.HIGHEST

parts = 6
early = (2,)
margin = 8
tile = 32


def reduction(count, part_ref, half_in, half_sum, piece_in, full, pair_send, pair_recv, peer_send, peer_recv, back_send, back_recv):
    rows = part_ref.shape[0]
    chips = count // 2
    half, piece = rows // 2, rows // count
    me = lax.axis_index("row")
    low, chip = lax.rem(me, 2), me // 2
    pair = me + 1 - 2 * low

    def other(step):
        return lax.rem(chip + step, chips)

    def copy_to(source, target, sends, recvs, slot, where):
        return pltpu.make_async_remote_copy(
            src_ref=source,
            dst_ref=target,
            send_sem=sends.at[slot],
            recv_sem=recvs.at[slot],
            device_id={"row": where},
            device_id_type=pl.DeviceIdType.MESH,
        )

    first = copy_to(
        part_ref.at[pl.ds(pl.multiple_of((1 - low) * half, 8), half)], half_in, pair_send, pair_recv, 0, pair
    )
    first.start()
    yield
    first.wait()
    half_sum[...] = part_ref[pl.ds(pl.multiple_of(low * half, 8), half)] + half_in[...]
    outgoing = [
        copy_to(
            half_sum.at[pl.ds(pl.multiple_of(other(step) * piece, 8), piece)],
            piece_in.at[step],
            peer_send,
            peer_recv,
            step,
            other(step) * 2 + low,
        )
        for step in range(1, chips)
    ]
    for copy in outgoing:
        copy.start()
    yield
    total = half_sum[pl.ds(pl.multiple_of(chip * piece, 8), piece)]
    for step, copy in enumerate(outgoing, 1):
        copy.wait()
        total = total + piece_in[step]
    mine = pl.ds(pl.multiple_of(low * half + chip * piece, 8), piece)
    full[mine] = total
    returning = [
        copy_to(full.at[mine], full.at[mine], back_send, back_recv, step, other(step) * 2 + low)
        for step in range(1, chips)
    ]
    for copy in returning:
        copy.start()
    yield
    for copy in returning:
        copy.wait()
    own_half = full.at[pl.ds(pl.multiple_of(low * half, 8), half)]
    last = copy_to(own_half, own_half, pair_send, pair_recv, 1, pair)
    last.start()
    yield
    last.wait()


def reduction_scratch(count, rows, cols):
    chips = count // 2
    return [
        pltpu.VMEM((rows, cols), jnp.float32),
        pltpu.VMEM((rows // 2, cols), jnp.float32),
        pltpu.VMEM((rows // 2, cols), jnp.float32),
        pltpu.VMEM((chips, rows // count, cols), jnp.float32),
        pltpu.VMEM((rows, cols), jnp.float32),
        pltpu.SemaphoreType.DMA((2,)),
        pltpu.SemaphoreType.DMA((2,)),
    ] + [pltpu.SemaphoreType.DMA((chips,))] * 4


def tile_inverse(block):
    shape = (tile, tile)
    row_ids = lax.broadcasted_iota(jnp.int32, shape, 0)
    col_ids = lax.broadcasted_iota(jnp.int32, shape, 1)
    right = (row_ids == col_ids).astype(jnp.float32)
    left = block
    scale = jnp.zeros(shape, jnp.float32)
    for start in range(0, tile, 8):
        columns = [
            jnp.broadcast_to(left[start:, start + k : start + k + 1], (tile - start, tile)) for k in range(8)
        ]
        below_left, below_right = left[start:], right[start:]
        ids = row_ids[start:]
        for j in range(8):
            pivot = columns[j][j : j + 1]
            factor = jnp.where(ids > start + j, columns[j] * (1.0 / pivot), 0.0)
            scale = jnp.where(row_ids == start + j, lax.rsqrt(pivot), scale)
            for k in range(j + 1, 8):
                columns[k] = columns[k] - factor * columns[k][j : j + 1]
            below_left = below_left - factor * below_left[j : j + 1]
            below_right = below_right - factor * below_right[j : j + 1]
        if start:
            left = jnp.concatenate([left[:start], below_left], axis=0)
            right = jnp.concatenate([right[:start], below_right], axis=0)
        else:
            left, right = below_left, below_right
    return right * scale


def mul(a, b, contract):
    return lax.dot_general(a, b, ((contract[0:1], contract[1:2]), ((), ())), precision=exact, preferred_element_type=jnp.float32)


def dot16(a, b, contract):
    return lax.dot_general(a, b, ((contract[0:1], contract[1:2]), ((), ())), preferred_element_type=jnp.float32)


def thirds(value):
    high = value.astype(jnp.bfloat16)
    value = value - high.astype(jnp.float32)
    mid = value.astype(jnp.bfloat16)
    return high, mid, (value - mid.astype(jnp.float32)).astype(jnp.bfloat16)


def packed(left, right):
    lh, lm, ll = thirds(left)
    rh, rm, rl = thirds(right)
    return dot16(
        jnp.concatenate([lh, lh, lm, lm, lh, ll], axis=0), jnp.concatenate([rh, rm, rh, rm, rl, rh], axis=0), (0, 0)
    )


def halves(value):
    high = value.astype(jnp.bfloat16)
    return high, (value - high.astype(jnp.float32)).astype(jnp.bfloat16)


def whole_kernel(
    count, coef_hbm, z_hbm, noise_hbm, bar_hbm, rbar_hbm, z_out, noise_out,
    coef_ref, rbar_ref, ahead_out, ahead_in,
    coef_rows, halo_rows, coefs, values, hop, second, first, partial, light, halo,
    noise_in, bar_in, result, all_high, all_low, acc_z, acc_n, work, weight_z, weight_n,
    load_sem, send_low, recv_low, send_high, recv_high, *sums,
):
    quads, rows, cells, cols = z_hbm.shape
    size = 2 * cols
    chunk = cells // parts
    strips = quads * rows
    block = strips * chunk
    me = lax.axis_index("row")
    has_low, has_high = me > 0, me < count - 1
    gram_scratch, cross_scratch = sums[:11], sums[11:]
    gram_part, gram_full = gram_scratch[0], gram_scratch[4]
    cross_part, cross_full = cross_scratch[0], cross_scratch[4]

    load_z = pltpu.make_async_copy(z_hbm, values.at[:, :, margin : margin + cells], load_sem.at[0])
    load_noise = pltpu.make_async_copy(noise_hbm, noise_in, load_sem.at[1])
    load_bar = pltpu.make_async_copy(bar_hbm, bar_in, load_sem.at[2])
    load_coef = pltpu.make_async_copy(coef_hbm, coef_ref, load_sem.at[3])
    load_rbar = pltpu.make_async_copy(rbar_hbm, rbar_ref, load_sem.at[4])
    load_coef.start()
    load_z.start()

    barrier = pltpu.get_barrier_semaphore()
    low, chip = lax.rem(me, 2), me // 2
    friends = [me + 1 - 2 * low]
    friends += [lax.rem(chip + step, count // 2) * 2 + low for step in range(1, count // 2)]

    @pl.when(has_low)
    def _():
        pl.semaphore_signal(barrier, inc=1, device_id={"row": me - 1}, device_id_type=pl.DeviceIdType.MESH)

    @pl.when(has_high)
    def _():
        pl.semaphore_signal(barrier, inc=1, device_id={"row": me + 1}, device_id_type=pl.DeviceIdType.MESH)

    for friend in friends:
        pl.semaphore_signal(barrier, inc=1, device_id={"row": friend}, device_id_type=pl.DeviceIdType.MESH)
    load_noise.start()
    load_bar.start()
    load_rbar.start()

    def link(source, target, slot, upward):
        sends, recvs = (send_high, recv_high) if upward else (send_low, recv_low)
        return pltpu.make_async_remote_copy(
            src_ref=source,
            dst_ref=target,
            send_sem=sends.at[slot],
            recv_sem=recvs.at[slot],
            device_id={"row": me + 1 if upward else me - 1},
            device_id_type=pl.DeviceIdType.MESH,
        )

    def message(source, padded, run, stage, piece, upward):
        offset = margin if padded else 0
        return link(
            source.at[0:2, rows - 1 if upward else 0, pl.ds(offset + piece * chunk, chunk)],
            halo.at[run, 0 if upward else 1, 2 * stage : 2 * stage + 2, pl.ds(piece * chunk, chunk)],
            (2 * run + stage) * parts + piece,
            upward,
        )

    def rates(upward):
        return link(coef_rows.at[8:16], halo_rows.at[0 if upward else 1], 4 * parts, upward)

    def ahead(slot, upward):
        return link(
            ahead_out.at[1 if upward else 0, slot], ahead_in.at[0 if upward else 1, slot], 4 * parts + 1 + slot, upward
        )

    def send(copy_of):
        @pl.when(has_high)
        def _():
            copy_of(True).start()

        @pl.when(has_low)
        def _():
            copy_of(False).start()

    def receive(copy_of):
        @pl.when(has_low)
        def _():
            copy_of(True).wait_recv()

        @pl.when(has_high)
        def _():
            copy_of(False).wait_recv()

    def sent(copy_of):
        @pl.when(has_high)
        def _():
            copy_of(True).wait_send()

        @pl.when(has_low)
        def _():
            copy_of(False).wait_send()

    def at(piece):
        return slice(piece * chunk, (piece + 1) * chunk)

    def inner(piece, shift=0):
        return slice(margin + piece * chunk + shift, margin + (piece + 1) * chunk + shift)

    def coef(kind, row, piece):
        return coefs[kind * rows + row, at(piece)]

    def strip(piece, quad, row):
        start = piece * block + (quad * rows + row) * chunk
        return slice(start, start + chunk)

    load_coef.wait()
    for kind in range(6):
        for row in range(rows):
            line = coef_ref[kind, row : row + 1] * jnp.float32(rate_scales[kind])
            coef_rows[kind * rows + row : kind * rows + row + 1] = line * jnp.float32(extra_scales[kind])
    coef_rows[12:16] = jnp.zeros((4, cells), jnp.float32)
    columns = coef_rows[...].T
    for index in range(6 * rows):
        coefs[index] = jnp.broadcast_to(columns[:, index : index + 1], (cells, cols))
    for buffer in (values, hop, second):
        for quad in range(2):
            for row in range(rows):
                buffer[quad, row, :margin] = jnp.zeros((margin, cols), jnp.float32)
                buffer[quad, row, margin + cells :] = jnp.zeros((margin, cols), jnp.float32)
    for side, has in enumerate((has_low, has_high)):

        @pl.when(jnp.logical_not(has))
        def _():
            halo[:, side] = jnp.zeros(halo.shape[:1] + halo.shape[2:], jnp.float32)
            halo_rows[side] = jnp.zeros(halo_rows.shape[1:], jnp.float32)

    def local(get, buffer, row, piece, transposed):
        xa, pa, xb, pb = [get(quad, row, piece) for quad in range(4)]
        detuning, mech, coupling, cavity, phonon, hopping = [coef(kind, row, piece) for kind in range(6)]
        hops = [
            buffer[quad, row, inner(piece, -1)] + buffer[quad, row, inner(piece, 1)] + buffer[quad, 1 - row, inner(piece)]
            for quad in range(2)
        ]
        if transposed:
            return (
                detuning * pa - cavity * xa - coupling * pb + hops[1],
                -detuning * xa - cavity * pa - hops[0],
                -coupling * pa - mech * pb,
                mech * xb - phonon * pb,
            )
        return (
            -cavity * xa - detuning * pa - hopping * hops[1],
            detuning * xa - cavity * pa - coupling * xb + hopping * hops[0],
            mech * pb,
            -mech * xb - phonon * pb - coupling * xa,
        )

    def value_at(quad, row, piece):
        return values[quad, row, inner(piece)]

    def first_at(quad, row, piece):
        return first[quad, row, at(piece)]

    def first_term(run, source, piece):
        for row in range(rows):
            for quad, value in enumerate(local(value_at, source, row, piece, run == 1)):
                first[quad, row, at(piece)] = value
                if quad < 2:
                    partial[quad, row, at(piece)] = coef(5, row, piece) * value if run else value
        if run == 0 or piece not in early:
            send(functools.partial(message, partial, False, run, 1, piece))

    def first_halo(run, source, piece):
        if run == 0 or piece not in early:
            receive(functools.partial(message, source, True, run, 0, piece))
        for row in range(rows):
            halo_x, halo_p = halo[run, row, 0, at(piece)], halo[run, row, 1, at(piece)]
            hopping = coef(5, row, piece)
            if run:
                new_x, new_p = first_at(0, row, piece) + halo_p, first_at(1, row, piece) - halo_x
            else:
                new_x = first_at(0, row, piece) - hopping * halo_p
                new_p = first_at(1, row, piece) + hopping * halo_x
            first[0, row, at(piece)] = new_x
            first[1, row, at(piece)] = new_p
            second[0, row, inner(piece)] = hopping * new_x if run else new_x
            second[1, row, inner(piece)] = hopping * new_p if run else new_p

    def second_term(run, row, piece):
        found = local(first_at, second, row, piece, run == 1)
        return [value_at(quad, row, piece) + first_at(quad, row, piece) + 0.5 * found[quad] for quad in range(4)]

    def last_halo(run, source, piece):
        if run == 0 or piece not in early:
            receive(functools.partial(message, partial, False, run, 1, piece))
        found = []
        for row in range(rows):
            beyond = coefs[6 * rows + row, at(piece)]
            own_x, own_p = source[0, row, inner(piece)], source[1, row, inner(piece)]
            halo_x, halo_p = halo[run, row, 2, at(piece)], halo[run, row, 3, at(piece)]
            if run:
                add_x, add_p = 0.5 * (halo_p - beyond * own_x), -0.5 * (halo_x + beyond * own_p)
            else:
                hopping = 0.5 * coef(5, row, piece)
                add_x, add_p = -hopping * (halo_p + beyond * own_x), hopping * (halo_x - beyond * own_p)
            found.append((add_x, add_p))
        return found

    pl.semaphore_wait(barrier, jnp.where(me > 0, 1, 0) + jnp.where(me < count - 1, 1, 0) + len(friends))
    send(rates)
    load_z.wait()
    for piece in range(parts):
        send(functools.partial(message, values, True, 0, 0, piece))
    for piece in range(parts):
        first_term(0, values, piece)

    load_noise.wait()
    load_bar.wait()
    for piece in range(parts):
        for quad in range(quads):
            for row in range(rows):
                where = strip(piece, quad, row)
                all_high[where, cols:size], all_low[where, cols:size] = halves(noise_in[quad, row, at(piece)])
                all_high[where, size:], all_low[where, size:] = halves(bar_in[quad, row, at(piece)])

    def accumulate(acc, start, stop, begin, fresh):
        lines = slice(start, stop)
        high = all_high[lines, begin : begin + cols]
        left = jnp.concatenate([high, all_low[lines, begin : begin + cols]], axis=1)
        both = dot16(left, all_high[lines, begin:], (0, 0))
        found = both[:cols] + both[cols:] + dot16(high, all_low[lines, begin:], (0, 0))
        acc[...] = found if fresh else acc[...] + found

    for piece in range(parts):
        accumulate(acc_n, piece * block, (piece + 1) * block, cols, piece == 0)

    receive(rates)
    sides = [halo_rows[0].T, halo_rows[1].T]
    for side in range(2):
        index = 10 - 8 + (rows - 1 if side == 0 else 0)
        coefs[6 * rows + side] = jnp.broadcast_to(sides[side][:, index : index + 1], (cells, cols))

    def finish(piece):
        for row in range(rows):
            found = second_term(0, row, piece)
            for quad in range(2):
                light[quad, row, at(piece)] = found[quad]
            for quad in range(2, 4):
                where = strip(piece, quad, row)
                all_high[where, :cols], all_low[where, :cols] = halves(found[quad])
            if piece in early:
                first[3, row, at(piece)] = found[3]
        accumulate(acc_z, piece * block + block // 2, (piece + 1) * block, 0, piece == 0)

    for piece in range(parts):
        first_halo(0, values, piece)
        if piece:
            finish(piece - 1)
    finish(parts - 1)
    for piece in range(parts):
        for row, added in enumerate(last_halo(0, values, piece)):
            for quad in range(2):
                where = strip(piece, quad, row)
                light[quad, row, at(piece)] = light[quad, row, at(piece)] + added[quad]
                all_high[where, :cols], all_low[where, :cols] = halves(light[quad, row, at(piece)])
        accumulate(acc_z, piece * block, piece * block + block // 2, 0, False)

    def fill_ahead():
        for slot, piece in enumerate(early):
            for row in range(rows):
                for part in range(4):

                    def get(quad, line, shift=0):
                        where = slice(piece * chunk + shift, (piece + 1) * chunk + shift)
                        if part == 0:
                            return first[3, line, where] if quad == 3 else light[quad, line, where]
                        if part == 1:
                            return noise_in[quad, line, where]
                        return bar_in[quad, line, where, (part - 2) * cols : (part - 1) * cols]

                    def hop_rate(shift):
                        return coefs[5 * rows + row, piece * chunk + shift : (piece + 1) * chunk + shift]

                    xa, pa, pb = get(0, row), get(1, row), get(3, row)
                    hops = [
                        hop_rate(-1) * get(quad, row, -1)
                        + hop_rate(1) * get(quad, row, 1)
                        + coef(5, 1 - row, piece) * get(quad, 1 - row)
                        for quad in range(2)
                    ]
                    detuning, coupling, cavity = [coef(kind, row, piece) for kind in (0, 2, 3)]
                    found_x = detuning * pa - cavity * xa - coupling * pb + hops[1]
                    found_p = -detuning * xa - cavity * pa - hops[0]
                    for plane, value in enumerate((xa, pa, found_x, found_p)):
                        ahead_out[row, slot, plane * chunk : (plane + 1) * chunk, part * cols : (part + 1) * cols] = (
                            hop_rate(0) * value
                        )

    gram_part[:cols] = acc_z[:, :cols]
    gram_part[cols:size] = acc_z[:, cols:size]
    gram_part[size : size + cols] = acc_n[:, :cols]
    if gram_part.shape[0] > size + cols:
        gram_part[size + cols :] = jnp.zeros((gram_part.shape[0] - size - cols, cols), jnp.float32)
    gram_steps = reduction(count, *gram_scratch)
    cross_steps = reduction(count, *cross_scratch)
    next(gram_steps)
    for part, (acc, begin) in enumerate(((acc_z, size), (acc_z, size + cols), (acc_n, cols), (acc_n, size))):
        cross_part[part * cols : (part + 1) * cols] = acc[:, begin : begin + cols]
    next(cross_steps)
    next(gram_steps)
    fill_ahead()
    for piece in range(parts):
        sent(functools.partial(message, values, True, 0, 0, piece))
        sent(functools.partial(message, partial, False, 0, 1, piece))
    sent(rates)
    next(gram_steps)
    next(cross_steps)
    next(gram_steps)
    next(cross_steps)
    next(gram_steps, None)
    for slot in range(len(early)):
        send(functools.partial(ahead, slot))

    row_ids = lax.broadcasted_iota(jnp.int32, (size, size), 0)
    col_ids = lax.broadcasted_iota(jnp.int32, (size, size), 1)
    work[:cols, :cols] = gram_full[:cols]
    work[:cols, cols:size] = gram_full[cols:size]
    work[cols:, :cols] = jnp.zeros((cols, cols), jnp.float32)
    work[cols:, cols:size] = gram_full[size : size + cols]
    work[:, size:] = (row_ids == col_ids).astype(jnp.float32)
    for start in range(0, size, tile):
        stop = start + tile
        small = tile_inverse(work[start:stop, start:stop])
        panel = packed(small.T, work[start:stop, :])
        work[start:stop, :] = panel
        if stop < size:
            base, end = stop // 128 * 128, size + (stop + 127) // 128 * 128
            update = packed(panel[:, base:size], panel[:, base:end])
            work[stop:, base:end] = work[stop:, base:end] - update[stop - base :]
        if start // tile in (4, 7):
            next(cross_steps, None)
    upper = jnp.where(row_ids <= col_ids, work[:, :size], 0.0)
    inverse = jnp.where(row_ids >= col_ids, work[:, size:], 0.0)
    load_rbar.wait()
    bar = jnp.where(row_ids <= col_ids, rbar_ref[...], 0.0)
    cross = jnp.concatenate(
        [
            jnp.concatenate([cross_full[:cols], cross_full[cols:size]], axis=1),
            jnp.concatenate([cross_full[size : size + cols], cross_full[size + cols :]], axis=1),
        ],
        axis=0,
    )
    middle = mul(upper, bar, (1, 1)) - mul(cross.T, inverse, (1, 1))
    symmetric = jnp.where(row_ids >= col_ids, middle, middle.T)
    mix = mul(inverse.T, mul(symmetric, inverse, (1, 0)), (1, 0))
    for begin, value in ((0, mix), (size, inverse)):
        lines = slice(begin, begin + size)
        high, rest = halves(value)
        weight_z[lines, :cols], weight_z[lines, cols:] = high[:, :cols], rest[:, :cols]
        weight_n[lines, :cols], weight_n[lines, cols:] = high[:, cols:], rest[:, cols:]

    def gradient(weight, piece):
        lines = slice(piece * block, (piece + 1) * block)
        both = dot16(all_high[lines], weight[...], (1, 0))
        return both[:, :cols] + both[:, cols:] + dot16(all_low[lines], weight[:, :cols], (1, 0))

    for piece in range(parts):
        grad = gradient(weight_z, piece)
        for quad in range(quads):
            for row in range(rows):
                start = (quad * rows + row) * chunk
                values[quad, row, inner(piece)] = grad[start : start + chunk]
                if quad < 2:
                    hop[quad, row, inner(piece)] = coef(5, row, piece) * grad[start : start + chunk]
        if piece not in early:
            send(functools.partial(message, hop, True, 1, 0, piece))
        if piece:
            first_term(1, hop, piece - 1)
    first_term(1, hop, parts - 1)
    for slot, piece in enumerate(early):
        for side, has in enumerate((has_low, has_high)):

            @pl.when(has)
            def _():
                ahead(slot, side == 0).wait_recv()
                high, rest = halves(ahead_in[side, slot])
                both = dot16(high, weight_z[...], (1, 0))
                edge = both[:, :cols] + both[:, cols:] + dot16(rest, weight_z[:, :cols], (1, 0))
                for plane in range(4):
                    halo[1, side, plane, at(piece)] = edge[plane * chunk : (plane + 1) * chunk]

    for piece in range(parts):
        grad = gradient(weight_n, piece)
        for quad in range(quads):
            for row in range(rows):
                start = (quad * rows + row) * chunk
                noise_in[quad, row, at(piece)] = grad[start : start + chunk]
    store_noise = pltpu.make_async_copy(noise_in, noise_out, load_sem.at[1])
    store_noise.start()

    def finish_back(piece):
        for row in range(rows):
            for quad, value in enumerate(second_term(1, row, piece)):
                result[quad, row, at(piece)] = value

    for piece in range(parts):
        first_halo(1, hop, piece)
        if piece:
            finish_back(piece - 1)
    finish_back(parts - 1)
    stores = [store_noise, pltpu.make_async_copy(result.at[2:4], z_out.at[2:4], load_sem.at[0])]
    stores[1].start()
    for piece in range(parts):
        for row, added in enumerate(last_halo(1, hop, piece)):
            for quad in range(2):
                result[quad, row, at(piece)] = result[quad, row, at(piece)] + added[quad]
        stores.append(pltpu.make_async_copy(result.at[0:2, :, at(piece)], z_out.at[0:2, :, at(piece)], load_sem.at[5 + piece]))
        stores[-1].start()
    for store in stores:
        store.wait()
    for slot in range(len(early)):
        sent(functools.partial(ahead, slot))
    for piece in range(parts):
        if piece not in early:
            sent(functools.partial(message, hop, True, 1, 0, piece))
            sent(functools.partial(message, partial, False, 1, 1, piece))


def on_device(cell_coeffs, z_factor, noise_cols, q_bar, r_bar):
    count = lax.axis_size("row")
    quads, rows, cells, cols = z_factor.shape
    size = 2 * cols
    total = quads * rows * cells
    unit = 8 * count
    gram_rows = (size + cols + unit - 1) // unit * unit
    padded = cells + 2 * margin
    plane = (cells, cols)
    far = pl.BlockSpec(memory_space=pl.ANY)

    def floats(*shape):
        return pltpu.VMEM(shape, jnp.float32)

    def shorts(*shape):
        return pltpu.VMEM(shape, jnp.bfloat16)

    return pl.pallas_call(
        functools.partial(whole_kernel, count),
        out_shape=(
            jax.ShapeDtypeStruct(z_factor.shape, jnp.float32),
            jax.ShapeDtypeStruct(noise_cols.shape, jnp.float32),
        ),
        in_specs=[far] * 5,
        out_specs=(far, far),
        scratch_shapes=[
            floats(*cell_coeffs.shape),
            floats(*r_bar.shape),
            floats(2, len(early), 4 * (cells // parts), 2 * size),
            floats(2, len(early), 4 * (cells // parts), 2 * size),
            floats(16, cells),
            floats(2, 8, cells),
            floats(6 * rows + 2, *plane),
            floats(quads, rows, padded, cols),
            floats(2, rows, padded, cols),
            floats(2, rows, padded, cols),
            floats(quads, rows, *plane),
            floats(2, rows, *plane),
            floats(2, rows, *plane),
            floats(2, 2, 4, *plane),
            floats(quads, rows, *plane),
            floats(quads, rows, cells, size),
            floats(quads, rows, *plane),
            shorts(total, 2 * size),
            shorts(total, 2 * size),
            floats(cols, 2 * size),
            floats(cols, 2 * size - cols),
            floats(size, 2 * size),
            shorts(2 * size, size),
            shorts(2 * size, size),
            pltpu.SemaphoreType.DMA((5 + parts,)),
        ]
        + [pltpu.SemaphoreType.DMA((4 * parts + 1 + len(early),))] * 4
        + reduction_scratch(count, gram_rows, cols)
        + reduction_scratch(count, 4 * cols, cols),
        compiler_params=pltpu.CompilerParams(
            collective_id=0, has_side_effects=True, vmem_limit_bytes=62 * 2**20
        ),
    )(cell_coeffs, z_factor, noise_cols, q_bar, r_bar)


def solution(mesh):
    return jax.shard_map(
        on_device,
        mesh=mesh,
        in_specs=(
            P(None, "row", None),
            P(None, ("grp", "row"), None, None),
            P(None, ("grp", "row"), None, None),
            P(None, ("grp", "row"), None, None),
            P("grp", None),
        ),
        out_specs=(P(None, ("grp", "row"), None, None), P(None, ("grp", "row"), None, None)),
        check_vma=False,
    )
```

```python
import functools

import jax
import jax.numpy as jnp
from jax import lax
from jax.experimental import pallas as pl
from jax.experimental.pallas import tpu as pltpu
from jax.sharding import PartitionSpec as P

rate_scales = (0.4, 0.4, 0.1, 0.2, 0.1, 0.1)
extra_scales = (1.0, 1.0, 2.0, 0.5, 0.5, 1.0)

parts = 6
early = (2,)
margin = 8
tile = 32


def reduction(count, part_ref, half_in, half_sum, piece_in, full, pair_send, pair_recv, peer_send, peer_recv, back_send, back_recv):
    rows = part_ref.shape[0]
    chips = count // 2
    half, piece = rows // 2, rows // count
    me = lax.axis_index("row")
    low, chip = lax.rem(me, 2), me // 2
    pair = me + 1 - 2 * low

    def other(step):
        return lax.rem(chip + step, chips)

    def copy_to(source, target, sends, recvs, slot, where):
        return pltpu.make_async_remote_copy(
            src_ref=source,
            dst_ref=target,
            send_sem=sends.at[slot],
            recv_sem=recvs.at[slot],
            device_id={"row": where},
            device_id_type=pl.DeviceIdType.MESH,
        )

    first = copy_to(
        part_ref.at[pl.ds(pl.multiple_of((1 - low) * half, 8), half)], half_in, pair_send, pair_recv, 0, pair
    )
    first.start()
    yield
    first.wait()
    half_sum[...] = part_ref[pl.ds(pl.multiple_of(low * half, 8), half)] + half_in[...]
    outgoing = [
        copy_to(
            half_sum.at[pl.ds(pl.multiple_of(other(step) * piece, 8), piece)],
            piece_in.at[step],
            peer_send,
            peer_recv,
            step,
            other(step) * 2 + low,
        )
        for step in range(1, chips)
    ]
    for copy in outgoing:
        copy.start()
    yield
    total = half_sum[pl.ds(pl.multiple_of(chip * piece, 8), piece)]
    for step, copy in enumerate(outgoing, 1):
        copy.wait()
        total = total + piece_in[step]
    mine = pl.ds(pl.multiple_of(low * half + chip * piece, 8), piece)
    full[mine] = total
    returning = [
        copy_to(full.at[mine], full.at[mine], back_send, back_recv, step, other(step) * 2 + low)
        for step in range(1, chips)
    ]
    for copy in returning:
        copy.start()
    yield
    for copy in returning:
        copy.wait()
    own_half = full.at[pl.ds(pl.multiple_of(low * half, 8), half)]
    last = copy_to(own_half, own_half, pair_send, pair_recv, 1, pair)
    last.start()
    yield
    last.wait()


def reduction_scratch(count, rows, cols):
    chips = count // 2
    return [
        pltpu.VMEM((rows, cols), jnp.float32),
        pltpu.VMEM((rows // 2, cols), jnp.float32),
        pltpu.VMEM((rows // 2, cols), jnp.float32),
        pltpu.VMEM((chips, rows // count, cols), jnp.float32),
        pltpu.VMEM((rows, cols), jnp.float32),
        pltpu.SemaphoreType.DMA((2,)),
        pltpu.SemaphoreType.DMA((2,)),
    ] + [pltpu.SemaphoreType.DMA((chips,))] * 4


def tile_inverse(block):
    shape = (tile, tile)
    row_ids = lax.broadcasted_iota(jnp.int32, shape, 0)
    col_ids = lax.broadcasted_iota(jnp.int32, shape, 1)
    right = (row_ids == col_ids).astype(jnp.float32)
    left = block
    scale = jnp.zeros(shape, jnp.float32)
    for start in range(0, tile, 8):
        columns = [
            jnp.broadcast_to(left[start:, start + k : start + k + 1], (tile - start, tile)) for k in range(8)
        ]
        below_left, below_right = left[start:], right[start:]
        ids = row_ids[start:]
        for j in range(8):
            pivot = columns[j][j : j + 1]
            factor = jnp.where(ids > start + j, columns[j] * (1.0 / pivot), 0.0)
            scale = jnp.where(row_ids == start + j, lax.rsqrt(pivot), scale)
            for k in range(j + 1, 8):
                columns[k] = columns[k] - factor * columns[k][j : j + 1]
            below_left = below_left - factor * below_left[j : j + 1]
            below_right = below_right - factor * below_right[j : j + 1]
        if start:
            left = jnp.concatenate([left[:start], below_left], axis=0)
            right = jnp.concatenate([right[:start], below_right], axis=0)
        else:
            left, right = below_left, below_right
    return right * scale


def dot16(a, b, contract):
    return lax.dot_general(a, b, ((contract[0:1], contract[1:2]), ((), ())), preferred_element_type=jnp.float32)


def thirds(value):
    high = value.astype(jnp.bfloat16)
    value = value - high.astype(jnp.float32)
    mid = value.astype(jnp.bfloat16)
    return high, mid, (value - mid.astype(jnp.float32)).astype(jnp.bfloat16)


def packed(left, right):
    lh, lm, ll = thirds(left)
    rh, rm, rl = thirds(right)
    return dot16(
        jnp.concatenate([lh, lh, lm, lm, lh, ll], axis=0), jnp.concatenate([rh, rm, rh, rm, rl, rh], axis=0), (0, 0)
    )


def high_mul(left, right, contract):
    (left_high, left_low), (right_high, right_low) = halves(left), halves(right)
    return dot16(left_high, right_high, contract) + (
        dot16(left_high, right_low, contract) + dot16(left_low, right_high, contract)
    )


def halves(value):
    high = value.astype(jnp.bfloat16)
    return high, (value - high.astype(jnp.float32)).astype(jnp.bfloat16)


def whole_kernel(
    count, coef_hbm, z_hbm, noise_hbm, bar_hbm, rbar_hbm, z_out, noise_out,
    coef_ref, rbar_ref, ahead_out, ahead_in,
    coef_rows, halo_rows, coefs, values, hop, second, first, partial, light, halo,
    noise_in, bar_in, result, all_high, all_low, acc_z, acc_n, work, weight_z, weight_n,
    load_sem, send_low, recv_low, send_high, recv_high, *sums,
):
    quads, rows, cells, cols = z_hbm.shape
    size = 2 * cols
    chunk = cells // parts
    strips = quads * rows
    block = strips * chunk
    me = lax.axis_index("row")
    has_low, has_high = me > 0, me < count - 1
    gram_scratch, cross_scratch = sums[:11], sums[11:]
    gram_part, gram_full = gram_scratch[0], gram_scratch[4]
    cross_part, cross_full = cross_scratch[0], cross_scratch[4]

    load_z = pltpu.make_async_copy(z_hbm, values.at[:, :, margin : margin + cells], load_sem.at[0])
    load_noise = pltpu.make_async_copy(noise_hbm, noise_in, load_sem.at[1])
    load_bar = pltpu.make_async_copy(bar_hbm, bar_in, load_sem.at[2])
    load_coef = pltpu.make_async_copy(coef_hbm, coef_ref, load_sem.at[3])
    load_rbar = pltpu.make_async_copy(rbar_hbm, rbar_ref, load_sem.at[4])
    load_coef.start()
    load_z.start()

    barrier = pltpu.get_barrier_semaphore()
    low, chip = lax.rem(me, 2), me // 2
    friends = [me + 1 - 2 * low]
    friends += [lax.rem(chip + step, count // 2) * 2 + low for step in range(1, count // 2)]

    @pl.when(has_low)
    def _():
        pl.semaphore_signal(barrier, inc=1, device_id={"row": me - 1}, device_id_type=pl.DeviceIdType.MESH)

    @pl.when(has_high)
    def _():
        pl.semaphore_signal(barrier, inc=1, device_id={"row": me + 1}, device_id_type=pl.DeviceIdType.MESH)

    for friend in friends:
        pl.semaphore_signal(barrier, inc=1, device_id={"row": friend}, device_id_type=pl.DeviceIdType.MESH)
    load_noise.start()
    load_bar.start()
    load_rbar.start()

    def link(source, target, slot, upward):
        sends, recvs = (send_high, recv_high) if upward else (send_low, recv_low)
        return pltpu.make_async_remote_copy(
            src_ref=source,
            dst_ref=target,
            send_sem=sends.at[slot],
            recv_sem=recvs.at[slot],
            device_id={"row": me + 1 if upward else me - 1},
            device_id_type=pl.DeviceIdType.MESH,
        )

    def message(source, padded, run, stage, piece, upward):
        offset = margin if padded else 0
        return link(
            source.at[0:2, rows - 1 if upward else 0, pl.ds(offset + piece * chunk, chunk)],
            halo.at[run, 0 if upward else 1, 2 * stage : 2 * stage + 2, pl.ds(piece * chunk, chunk)],
            (2 * run + stage) * parts + piece,
            upward,
        )

    def rates(upward):
        return link(coef_rows.at[8:16], halo_rows.at[0 if upward else 1], 4 * parts, upward)

    def ahead(slot, upward):
        return link(
            ahead_out.at[1 if upward else 0, slot], ahead_in.at[0 if upward else 1, slot], 4 * parts + 1 + slot, upward
        )

    def send(copy_of):
        @pl.when(has_high)
        def _():
            copy_of(True).start()

        @pl.when(has_low)
        def _():
            copy_of(False).start()

    def receive(copy_of):
        @pl.when(has_low)
        def _():
            copy_of(True).wait_recv()

        @pl.when(has_high)
        def _():
            copy_of(False).wait_recv()

    def sent(copy_of):
        @pl.when(has_high)
        def _():
            copy_of(True).wait_send()

        @pl.when(has_low)
        def _():
            copy_of(False).wait_send()

    def at(piece):
        return slice(piece * chunk, (piece + 1) * chunk)

    def inner(piece, shift=0):
        return slice(margin + piece * chunk + shift, margin + (piece + 1) * chunk + shift)

    def coef(kind, row, piece):
        return coefs[kind * rows + row, at(piece)]

    def strip(piece, quad, row):
        start = piece * block + (quad * rows + row) * chunk
        return slice(start, start + chunk)

    load_coef.wait()
    for kind in range(6):
        for row in range(rows):
            line = coef_ref[kind, row : row + 1] * jnp.float32(rate_scales[kind])
            coef_rows[kind * rows + row : kind * rows + row + 1] = line * jnp.float32(extra_scales[kind])
    coef_rows[12:16] = jnp.zeros((4, cells), jnp.float32)
    columns = coef_rows[...].T
    for index in range(6 * rows):
        coefs[index] = jnp.broadcast_to(columns[:, index : index + 1], (cells, cols))
    for buffer in (values, hop, second):
        for quad in range(2):
            for row in range(rows):
                buffer[quad, row, :margin] = jnp.zeros((margin, cols), jnp.float32)
                buffer[quad, row, margin + cells :] = jnp.zeros((margin, cols), jnp.float32)
    for side, has in enumerate((has_low, has_high)):

        @pl.when(jnp.logical_not(has))
        def _():
            halo[:, side] = jnp.zeros(halo.shape[:1] + halo.shape[2:], jnp.float32)
            halo_rows[side] = jnp.zeros(halo_rows.shape[1:], jnp.float32)

    def local(get, buffer, row, piece, transposed):
        xa, pa, xb, pb = [get(quad, row, piece) for quad in range(4)]
        detuning, mech, coupling, cavity, phonon, hopping = [coef(kind, row, piece) for kind in range(6)]
        hops = [
            buffer[quad, row, inner(piece, -1)] + buffer[quad, row, inner(piece, 1)] + buffer[quad, 1 - row, inner(piece)]
            for quad in range(2)
        ]
        if transposed:
            return (
                detuning * pa - cavity * xa - coupling * pb + hops[1],
                -detuning * xa - cavity * pa - hops[0],
                -coupling * pa - mech * pb,
                mech * xb - phonon * pb,
            )
        return (
            -cavity * xa - detuning * pa - hopping * hops[1],
            detuning * xa - cavity * pa - coupling * xb + hopping * hops[0],
            mech * pb,
            -mech * xb - phonon * pb - coupling * xa,
        )

    def value_at(quad, row, piece):
        return values[quad, row, inner(piece)]

    def first_at(quad, row, piece):
        return first[quad, row, at(piece)]

    def first_term(run, source, piece):
        for row in range(rows):
            for quad, value in enumerate(local(value_at, source, row, piece, run == 1)):
                first[quad, row, at(piece)] = value
                if quad < 2:
                    partial[quad, row, at(piece)] = coef(5, row, piece) * value if run else value
        if run == 0 or piece not in early:
            send(functools.partial(message, partial, False, run, 1, piece))

    def first_halo(run, source, piece):
        if run == 0 or piece not in early:
            receive(functools.partial(message, source, True, run, 0, piece))
        for row in range(rows):
            halo_x, halo_p = halo[run, row, 0, at(piece)], halo[run, row, 1, at(piece)]
            hopping = coef(5, row, piece)
            if run:
                new_x, new_p = first_at(0, row, piece) + halo_p, first_at(1, row, piece) - halo_x
            else:
                new_x = first_at(0, row, piece) - hopping * halo_p
                new_p = first_at(1, row, piece) + hopping * halo_x
            first[0, row, at(piece)] = new_x
            first[1, row, at(piece)] = new_p
            second[0, row, inner(piece)] = hopping * new_x if run else new_x
            second[1, row, inner(piece)] = hopping * new_p if run else new_p

    def second_term(run, row, piece):
        found = local(first_at, second, row, piece, run == 1)
        return [value_at(quad, row, piece) + first_at(quad, row, piece) + 0.5 * found[quad] for quad in range(4)]

    def last_halo(run, source, piece):
        if run == 0 or piece not in early:
            receive(functools.partial(message, partial, False, run, 1, piece))
        found = []
        for row in range(rows):
            beyond = coefs[6 * rows + row, at(piece)]
            own_x, own_p = source[0, row, inner(piece)], source[1, row, inner(piece)]
            halo_x, halo_p = halo[run, row, 2, at(piece)], halo[run, row, 3, at(piece)]
            if run:
                add_x, add_p = 0.5 * (halo_p - beyond * own_x), -0.5 * (halo_x + beyond * own_p)
            else:
                hopping = 0.5 * coef(5, row, piece)
                add_x, add_p = -hopping * (halo_p + beyond * own_x), hopping * (halo_x - beyond * own_p)
            found.append((add_x, add_p))
        return found

    pl.semaphore_wait(barrier, jnp.where(me > 0, 1, 0) + jnp.where(me < count - 1, 1, 0) + len(friends))
    send(rates)
    load_z.wait()
    for piece in range(parts):
        send(functools.partial(message, values, True, 0, 0, piece))
    for piece in range(parts):
        first_term(0, values, piece)

    load_noise.wait()
    load_bar.wait()
    for piece in range(parts):
        for quad in range(quads):
            for row in range(rows):
                where = strip(piece, quad, row)
                all_high[where, cols:size], all_low[where, cols:size] = halves(noise_in[quad, row, at(piece)])
                all_high[where, size:], all_low[where, size:] = halves(bar_in[quad, row, at(piece)])

    def accumulate(acc, start, stop, begin, fresh):
        lines = slice(start, stop)
        high = all_high[lines, begin : begin + cols]
        left = jnp.concatenate([high, all_low[lines, begin : begin + cols]], axis=1)
        both = dot16(left, all_high[lines, begin:], (0, 0))
        found = both[:cols] + both[cols:] + dot16(high, all_low[lines, begin:], (0, 0))
        acc[...] = found if fresh else acc[...] + found

    for piece in range(parts):
        accumulate(acc_n, piece * block, (piece + 1) * block, cols, piece == 0)

    receive(rates)
    sides = [halo_rows[0].T, halo_rows[1].T]
    for side in range(2):
        index = 10 - 8 + (rows - 1 if side == 0 else 0)
        coefs[6 * rows + side] = jnp.broadcast_to(sides[side][:, index : index + 1], (cells, cols))

    def finish(piece):
        for row in range(rows):
            found = second_term(0, row, piece)
            for quad in range(2):
                light[quad, row, at(piece)] = found[quad]
            for quad in range(2, 4):
                where = strip(piece, quad, row)
                all_high[where, :cols], all_low[where, :cols] = halves(found[quad])
            if piece in early:
                first[3, row, at(piece)] = found[3]
        accumulate(acc_z, piece * block + block // 2, (piece + 1) * block, 0, piece == 0)

    for piece in range(parts):
        first_halo(0, values, piece)
        if piece:
            finish(piece - 1)
    finish(parts - 1)
    for piece in range(parts):
        for row, added in enumerate(last_halo(0, values, piece)):
            for quad in range(2):
                where = strip(piece, quad, row)
                light[quad, row, at(piece)] = light[quad, row, at(piece)] + added[quad]
                all_high[where, :cols], all_low[where, :cols] = halves(light[quad, row, at(piece)])
        accumulate(acc_z, piece * block, piece * block + block // 2, 0, False)

    def fill_ahead():
        for slot, piece in enumerate(early):
            for row in range(rows):
                for part in range(4):

                    def get(quad, line, shift=0):
                        where = slice(piece * chunk + shift, (piece + 1) * chunk + shift)
                        if part == 0:
                            return first[3, line, where] if quad == 3 else light[quad, line, where]
                        if part == 1:
                            return noise_in[quad, line, where]
                        return bar_in[quad, line, where, (part - 2) * cols : (part - 1) * cols]

                    def hop_rate(shift):
                        return coefs[5 * rows + row, piece * chunk + shift : (piece + 1) * chunk + shift]

                    xa, pa, pb = get(0, row), get(1, row), get(3, row)
                    hops = [
                        hop_rate(-1) * get(quad, row, -1)
                        + hop_rate(1) * get(quad, row, 1)
                        + coef(5, 1 - row, piece) * get(quad, 1 - row)
                        for quad in range(2)
                    ]
                    detuning, coupling, cavity = [coef(kind, row, piece) for kind in (0, 2, 3)]
                    found_x = detuning * pa - cavity * xa - coupling * pb + hops[1]
                    found_p = -detuning * xa - cavity * pa - hops[0]
                    for plane, value in enumerate((xa, pa, found_x, found_p)):
                        ahead_out[row, slot, plane * chunk : (plane + 1) * chunk, part * cols : (part + 1) * cols] = (
                            hop_rate(0) * value
                        )

    gram_part[:cols] = acc_z[:, :cols]
    gram_part[cols:size] = acc_z[:, cols:size]
    gram_part[size : size + cols] = acc_n[:, :cols]
    if gram_part.shape[0] > size + cols:
        gram_part[size + cols :] = jnp.zeros((gram_part.shape[0] - size - cols, cols), jnp.float32)
    gram_steps = reduction(count, *gram_scratch)
    cross_steps = reduction(count, *cross_scratch)
    next(gram_steps)
    for part, (acc, begin) in enumerate(((acc_z, size), (acc_z, size + cols), (acc_n, cols), (acc_n, size))):
        cross_part[part * cols : (part + 1) * cols] = acc[:, begin : begin + cols]
    next(cross_steps)
    next(gram_steps)
    fill_ahead()
    for piece in range(parts):
        sent(functools.partial(message, values, True, 0, 0, piece))
        sent(functools.partial(message, partial, False, 0, 1, piece))
    sent(rates)
    next(gram_steps)
    next(cross_steps)
    next(gram_steps)
    next(cross_steps)
    next(gram_steps, None)
    for slot in range(len(early)):
        send(functools.partial(ahead, slot))

    row_ids = lax.broadcasted_iota(jnp.int32, (size, size), 0)
    col_ids = lax.broadcasted_iota(jnp.int32, (size, size), 1)
    work[:cols, :cols] = gram_full[:cols]
    work[:cols, cols:size] = gram_full[cols:size]
    work[cols:, :cols] = jnp.zeros((cols, cols), jnp.float32)
    work[cols:, cols:size] = gram_full[size : size + cols]
    work[:, size:] = (row_ids == col_ids).astype(jnp.float32)
    for start in range(0, size, tile):
        stop = start + tile
        small = tile_inverse(work[start:stop, start:stop])
        panel = packed(small.T, work[start:stop, :])
        work[start:stop, :] = panel
        if stop < size:
            base, end = stop // 128 * 128, size + (stop + 127) // 128 * 128
            update = packed(panel[:, base:size], panel[:, base:end])
            work[stop:, base:end] = work[stop:, base:end] - update[stop - base :]
        if start // tile in (4, 7):
            next(cross_steps, None)
    upper = jnp.where(row_ids <= col_ids, work[:, :size], 0.0)
    inverse = jnp.where(row_ids >= col_ids, work[:, size:], 0.0)
    load_rbar.wait()
    bar = jnp.where(row_ids <= col_ids, rbar_ref[...], 0.0)
    cross = jnp.concatenate(
        [
            jnp.concatenate([cross_full[:cols], cross_full[cols:size]], axis=1),
            jnp.concatenate([cross_full[size : size + cols], cross_full[size + cols :]], axis=1),
        ],
        axis=0,
    )
    middle = high_mul(upper, bar, (1, 1)) - high_mul(cross.T, inverse, (1, 1))
    symmetric = jnp.where(row_ids >= col_ids, middle, middle.T)
    mix = high_mul(inverse.T, high_mul(symmetric, inverse, (1, 0)), (1, 0))
    for begin, value in ((0, mix), (size, inverse)):
        lines = slice(begin, begin + size)
        high, rest = halves(value)
        weight_z[lines, :cols], weight_z[lines, cols:] = high[:, :cols], rest[:, :cols]
        weight_n[lines, :cols], weight_n[lines, cols:] = high[:, cols:], rest[:, cols:]

    def gradient(weight, piece):
        lines = slice(piece * block, (piece + 1) * block)
        both = dot16(all_high[lines], weight[...], (1, 0))
        return both[:, :cols] + both[:, cols:] + dot16(all_low[lines], weight[:, :cols], (1, 0))

    for piece in range(parts):
        grad = gradient(weight_z, piece)
        for quad in range(quads):
            for row in range(rows):
                start = (quad * rows + row) * chunk
                values[quad, row, inner(piece)] = grad[start : start + chunk]
                if quad < 2:
                    hop[quad, row, inner(piece)] = coef(5, row, piece) * grad[start : start + chunk]
        if piece not in early:
            send(functools.partial(message, hop, True, 1, 0, piece))
        if piece:
            first_term(1, hop, piece - 1)
    first_term(1, hop, parts - 1)
    for slot, piece in enumerate(early):
        for side, has in enumerate((has_low, has_high)):

            @pl.when(has)
            def _():
                ahead(slot, side == 0).wait_recv()
                high, rest = halves(ahead_in[side, slot])
                both = dot16(high, weight_z[...], (1, 0))
                edge = both[:, :cols] + both[:, cols:] + dot16(rest, weight_z[:, :cols], (1, 0))
                for plane in range(4):
                    halo[1, side, plane, at(piece)] = edge[plane * chunk : (plane + 1) * chunk]

    for piece in range(parts):
        grad = gradient(weight_n, piece)
        for quad in range(quads):
            for row in range(rows):
                start = (quad * rows + row) * chunk
                noise_in[quad, row, at(piece)] = grad[start : start + chunk]
    store_noise = pltpu.make_async_copy(noise_in, noise_out, load_sem.at[1])
    store_noise.start()

    def finish_back(piece):
        for row in range(rows):
            for quad, value in enumerate(second_term(1, row, piece)):
                result[quad, row, at(piece)] = value

    for piece in range(parts):
        first_halo(1, hop, piece)
        if piece:
            finish_back(piece - 1)
    finish_back(parts - 1)
    stores = [store_noise, pltpu.make_async_copy(result.at[2:4], z_out.at[2:4], load_sem.at[0])]
    stores[1].start()
    for piece in range(parts):
        for row, added in enumerate(last_halo(1, hop, piece)):
            for quad in range(2):
                result[quad, row, at(piece)] = result[quad, row, at(piece)] + added[quad]
        stores.append(pltpu.make_async_copy(result.at[0:2, :, at(piece)], z_out.at[0:2, :, at(piece)], load_sem.at[5 + piece]))
        stores[-1].start()
    for store in stores:
        store.wait()
    for slot in range(len(early)):
        sent(functools.partial(ahead, slot))
    for piece in range(parts):
        if piece not in early:
            sent(functools.partial(message, hop, True, 1, 0, piece))
            sent(functools.partial(message, partial, False, 1, 1, piece))


def place_kernel(z_ref, noise_ref, z_out, noise_out, held, load_sem, store_sem):
    quads = z_ref.shape[0]
    loads, stores = [], []
    for index, (source, target) in enumerate(((z_ref, z_out), (noise_ref, noise_out))):
        for quad in range(quads):
            slot = index * quads + quad
            loads.append(pltpu.make_async_copy(source.at[quad], held.at[slot], load_sem.at[slot]))
            stores.append(pltpu.make_async_copy(held.at[slot], target.at[quad], store_sem.at[slot]))
    for load in loads:
        load.start()
    for load, store in zip(loads, stores):
        load.wait()
        store.start()
    for store in stores:
        store.wait()


def place(z_grad, noise_grad):
    far = pl.BlockSpec(memory_space=pl.ANY)
    count = 2 * z_grad.shape[0]
    return pl.pallas_call(
        place_kernel,
        out_shape=tuple(jax.ShapeDtypeStruct(value.shape, value.dtype) for value in (z_grad, noise_grad)),
        in_specs=[far, far],
        out_specs=(far, far),
        scratch_shapes=[
            pltpu.VMEM((count,) + z_grad.shape[1:], jnp.float32),
            pltpu.SemaphoreType.DMA((count,)),
            pltpu.SemaphoreType.DMA((count,)),
        ],
        compiler_params=pltpu.CompilerParams(vmem_limit_bytes=62 * 2**20),
    )(z_grad, noise_grad)


def on_device(cell_coeffs, z_factor, noise_cols, q_bar, r_bar):
    count = lax.axis_size("row")
    quads, rows, cells, cols = z_factor.shape
    size = 2 * cols
    total = quads * rows * cells
    unit = 8 * count
    gram_rows = (size + cols + unit - 1) // unit * unit
    padded = cells + 2 * margin
    plane = (cells, cols)
    far = pl.BlockSpec(memory_space=pl.ANY)

    def floats(*shape):
        return pltpu.VMEM(shape, jnp.float32)

    def shorts(*shape):
        return pltpu.VMEM(shape, jnp.bfloat16)

    z_grad, noise_grad = pl.pallas_call(
        functools.partial(whole_kernel, count),
        out_shape=(
            jax.ShapeDtypeStruct(z_factor.shape, jnp.float32),
            jax.ShapeDtypeStruct(noise_cols.shape, jnp.float32),
        ),
        in_specs=[far] * 5,
        out_specs=(far, far),
        scratch_shapes=[
            floats(*cell_coeffs.shape),
            floats(*r_bar.shape),
            floats(2, len(early), 4 * (cells // parts), 2 * size),
            floats(2, len(early), 4 * (cells // parts), 2 * size),
            floats(16, cells),
            floats(2, 8, cells),
            floats(6 * rows + 2, *plane),
            floats(quads, rows, padded, cols),
            floats(2, rows, padded, cols),
            floats(2, rows, padded, cols),
            floats(quads, rows, *plane),
            floats(2, rows, *plane),
            floats(2, rows, *plane),
            floats(2, 2, 4, *plane),
            floats(quads, rows, *plane),
            floats(quads, rows, cells, size),
            floats(quads, rows, *plane),
            shorts(total, 2 * size),
            shorts(total, 2 * size),
            floats(cols, 2 * size),
            floats(cols, 2 * size - cols),
            floats(size, 2 * size),
            shorts(2 * size, size),
            shorts(2 * size, size),
            pltpu.SemaphoreType.DMA((5 + parts,)),
        ]
        + [pltpu.SemaphoreType.DMA((4 * parts + 1 + len(early),))] * 4
        + reduction_scratch(count, gram_rows, cols)
        + reduction_scratch(count, 4 * cols, cols),
        compiler_params=pltpu.CompilerParams(
            collective_id=0, has_side_effects=True, vmem_limit_bytes=62 * 2**20
        ),
    )(cell_coeffs, z_factor, noise_cols, q_bar, r_bar)
    return place(z_grad, noise_grad)


def solution(mesh):
    return jax.shard_map(
        on_device,
        mesh=mesh,
        in_specs=(
            P(None, "row", None),
            P(None, ("grp", "row"), None, None),
            P(None, ("grp", "row"), None, None),
            P(None, ("grp", "row"), None, None),
            P("grp", None),
        ),
        out_specs=(P(None, ("grp", "row"), None, None), P(None, ("grp", "row"), None, None)),
        check_vma=False,
    )
```

```python
import functools

import jax
import jax.numpy as jnp
from jax import lax
from jax.experimental import pallas as pl
from jax.experimental.pallas import tpu as pltpu
from jax.sharding import PartitionSpec as P

rate_scales = (0.4, 0.4, 0.1, 0.2, 0.1, 0.1)
extra_scales = (1.0, 1.0, 2.0, 0.5, 0.5, 1.0)

parts = 6
early = (1,)
margin = 8
tile = 32


def reduction(count, part_ref, half_in, half_sum, piece_in, full, pair_send, pair_recv, peer_send, peer_recv, back_send, back_recv):
    rows = part_ref.shape[0]
    chips = count // 2
    half, piece = rows // 2, rows // count
    me = lax.axis_index("row")
    low, chip = lax.rem(me, 2), me // 2
    pair = me + 1 - 2 * low

    def other(step):
        return lax.rem(chip + step, chips)

    def copy_to(source, target, sends, recvs, slot, where):
        return pltpu.make_async_remote_copy(
            src_ref=source,
            dst_ref=target,
            send_sem=sends.at[slot],
            recv_sem=recvs.at[slot],
            device_id={"row": where},
            device_id_type=pl.DeviceIdType.MESH,
        )

    first = copy_to(
        part_ref.at[pl.ds(pl.multiple_of((1 - low) * half, 8), half)], half_in, pair_send, pair_recv, 0, pair
    )
    first.start()
    yield
    first.wait()
    half_sum[...] = part_ref[pl.ds(pl.multiple_of(low * half, 8), half)] + half_in[...]
    outgoing = [
        copy_to(
            half_sum.at[pl.ds(pl.multiple_of(other(step) * piece, 8), piece)],
            piece_in.at[step],
            peer_send,
            peer_recv,
            step,
            other(step) * 2 + low,
        )
        for step in range(1, chips)
    ]
    for copy in outgoing:
        copy.start()
    yield
    total = half_sum[pl.ds(pl.multiple_of(chip * piece, 8), piece)]
    for step, copy in enumerate(outgoing, 1):
        copy.wait()
        total = total + piece_in[step]
    mine = pl.ds(pl.multiple_of(low * half + chip * piece, 8), piece)
    full[mine] = total
    returning = [
        copy_to(full.at[mine], full.at[mine], back_send, back_recv, step, other(step) * 2 + low)
        for step in range(1, chips)
    ]
    for copy in returning:
        copy.start()
    yield
    for copy in returning:
        copy.wait()
    own_half = full.at[pl.ds(pl.multiple_of(low * half, 8), half)]
    last = copy_to(own_half, own_half, pair_send, pair_recv, 1, pair)
    last.start()
    yield
    last.wait()


def reduction_scratch(count, rows, cols):
    chips = count // 2
    return [
        pltpu.VMEM((rows, cols), jnp.float32),
        pltpu.VMEM((rows // 2, cols), jnp.float32),
        pltpu.VMEM((rows // 2, cols), jnp.float32),
        pltpu.VMEM((chips, rows // count, cols), jnp.float32),
        pltpu.VMEM((rows, cols), jnp.float32),
        pltpu.SemaphoreType.DMA((2,)),
        pltpu.SemaphoreType.DMA((2,)),
    ] + [pltpu.SemaphoreType.DMA((chips,))] * 4


def tile_inverse(block):
    shape = (tile, tile)
    row_ids = lax.broadcasted_iota(jnp.int32, shape, 0)
    col_ids = lax.broadcasted_iota(jnp.int32, shape, 1)
    right = (row_ids == col_ids).astype(jnp.float32)
    left = block
    scale = jnp.zeros(shape, jnp.float32)
    for start in range(0, tile, 8):
        columns = [
            jnp.broadcast_to(left[start:, start + k : start + k + 1], (tile - start, tile)) for k in range(8)
        ]
        below_left, below_right = left[start:], right[start:]
        ids = row_ids[start:]
        for j in range(8):
            pivot = columns[j][j : j + 1]
            factor = jnp.where(ids > start + j, columns[j] * (1.0 / pivot), 0.0)
            scale = jnp.where(row_ids == start + j, lax.rsqrt(pivot), scale)
            for k in range(j + 1, 8):
                columns[k] = columns[k] - factor * columns[k][j : j + 1]
            below_left = below_left - factor * below_left[j : j + 1]
            below_right = below_right - factor * below_right[j : j + 1]
        if start:
            left = jnp.concatenate([left[:start], below_left], axis=0)
            right = jnp.concatenate([right[:start], below_right], axis=0)
        else:
            left, right = below_left, below_right
    return right * scale


def dot16(a, b, contract):
    return lax.dot_general(a, b, ((contract[0:1], contract[1:2]), ((), ())), preferred_element_type=jnp.float32)


def thirds(value):
    high = value.astype(jnp.bfloat16)
    value = value - high.astype(jnp.float32)
    mid = value.astype(jnp.bfloat16)
    return high, mid, (value - mid.astype(jnp.float32)).astype(jnp.bfloat16)


def packed(left, right):
    lh, lm, ll = thirds(left)
    rh, rm, rl = thirds(right)
    return dot16(
        jnp.concatenate([lh, lh, lm, lm, lh, ll], axis=0), jnp.concatenate([rh, rm, rh, rm, rl, rh], axis=0), (0, 0)
    )


def high_mul(left, right, contract):
    (left_high, left_low), (right_high, right_low) = halves(left), halves(right)
    return dot16(left_high, right_high, contract) + (
        dot16(left_high, right_low, contract) + dot16(left_low, right_high, contract)
    )


def packed_rows(left, right):
    lh, lm, ll = thirds(left)
    rh, rm, rl = thirds(right)
    return dot16(
        jnp.concatenate([lh, lh, lm, lm, lh, ll], axis=1), jnp.concatenate([rh, rm, rh, rm, rl, rh], axis=0), (1, 0)
    )


def halves(value):
    high = value.astype(jnp.bfloat16)
    return high, (value - high.astype(jnp.float32)).astype(jnp.bfloat16)


def whole_kernel(
    count, coef_hbm, z_hbm, noise_hbm, bar_hbm, rbar_hbm, z_out, noise_out,
    coef_ref, rbar_ref, ahead_out, ahead_in,
    coef_rows, halo_rows, coefs, values, hop, second, first, partial, light, halo,
    noise_in, bar_in, result, all_high, all_low, acc_z, acc_n, work, weight_z, weight_n,
    load_sem, send_low, recv_low, send_high, recv_high, *sums,
):
    quads, rows, cells, cols = z_hbm.shape
    size = 2 * cols
    chunk = cells // parts
    strips = quads * rows
    block = strips * chunk
    me = lax.axis_index("row")
    has_low, has_high = me > 0, me < count - 1
    gram_scratch, cross_scratch = sums[:11], sums[11:]
    gram_part, gram_full = gram_scratch[0], gram_scratch[4]
    cross_part, cross_full = cross_scratch[0], cross_scratch[4]

    load_z = pltpu.make_async_copy(z_hbm, values.at[:, :, margin : margin + cells], load_sem.at[0])
    load_noise = pltpu.make_async_copy(noise_hbm, noise_in, load_sem.at[1])
    load_bar = pltpu.make_async_copy(bar_hbm, bar_in, load_sem.at[2])
    load_coef = pltpu.make_async_copy(coef_hbm, coef_ref, load_sem.at[3])
    load_rbar = pltpu.make_async_copy(rbar_hbm, rbar_ref, load_sem.at[4])
    load_coef.start()
    load_z.start()

    barrier = pltpu.get_barrier_semaphore()
    low, chip = lax.rem(me, 2), me // 2
    friends = [me + 1 - 2 * low]
    friends += [lax.rem(chip + step, count // 2) * 2 + low for step in range(1, count // 2)]

    @pl.when(has_low)
    def _():
        pl.semaphore_signal(barrier, inc=1, device_id={"row": me - 1}, device_id_type=pl.DeviceIdType.MESH)

    @pl.when(has_high)
    def _():
        pl.semaphore_signal(barrier, inc=1, device_id={"row": me + 1}, device_id_type=pl.DeviceIdType.MESH)

    for friend in friends:
        pl.semaphore_signal(barrier, inc=1, device_id={"row": friend}, device_id_type=pl.DeviceIdType.MESH)
    load_noise.start()
    load_bar.start()
    load_rbar.start()

    def link(source, target, slot, upward):
        sends, recvs = (send_high, recv_high) if upward else (send_low, recv_low)
        return pltpu.make_async_remote_copy(
            src_ref=source,
            dst_ref=target,
            send_sem=sends.at[slot],
            recv_sem=recvs.at[slot],
            device_id={"row": me + 1 if upward else me - 1},
            device_id_type=pl.DeviceIdType.MESH,
        )

    def message(source, padded, run, stage, piece, upward):
        offset = margin if padded else 0
        return link(
            source.at[0:2, rows - 1 if upward else 0, pl.ds(offset + piece * chunk, chunk)],
            halo.at[run, 0 if upward else 1, 2 * stage : 2 * stage + 2, pl.ds(piece * chunk, chunk)],
            (2 * run + stage) * parts + piece,
            upward,
        )

    def rates(upward):
        return link(coef_rows.at[8:16], halo_rows.at[0 if upward else 1], 4 * parts, upward)

    def ahead(slot, upward):
        return link(
            ahead_out.at[1 if upward else 0, slot], ahead_in.at[0 if upward else 1, slot], 4 * parts + 1 + slot, upward
        )

    def send(copy_of):
        @pl.when(has_high)
        def _():
            copy_of(True).start()

        @pl.when(has_low)
        def _():
            copy_of(False).start()

    def receive(copy_of):
        @pl.when(has_low)
        def _():
            copy_of(True).wait_recv()

        @pl.when(has_high)
        def _():
            copy_of(False).wait_recv()

    def sent(copy_of):
        @pl.when(has_high)
        def _():
            copy_of(True).wait_send()

        @pl.when(has_low)
        def _():
            copy_of(False).wait_send()

    def at(piece):
        return slice(piece * chunk, (piece + 1) * chunk)

    def inner(piece, shift=0):
        return slice(margin + piece * chunk + shift, margin + (piece + 1) * chunk + shift)

    def coef(kind, row, piece):
        return coefs[kind * rows + row, at(piece)]

    def strip(piece, quad, row):
        start = piece * block + (quad * rows + row) * chunk
        return slice(start, start + chunk)

    load_coef.wait()
    for kind in range(6):
        for row in range(rows):
            line = coef_ref[kind, row : row + 1] * jnp.float32(rate_scales[kind])
            coef_rows[kind * rows + row : kind * rows + row + 1] = line * jnp.float32(extra_scales[kind])
    coef_rows[12:16] = jnp.zeros((4, cells), jnp.float32)
    columns = coef_rows[...].T
    for index in range(6 * rows):
        coefs[index] = jnp.broadcast_to(columns[:, index : index + 1], (cells, cols))
    for buffer in (values, hop, second):
        for quad in range(2):
            for row in range(rows):
                buffer[quad, row, :margin] = jnp.zeros((margin, cols), jnp.float32)
                buffer[quad, row, margin + cells :] = jnp.zeros((margin, cols), jnp.float32)
    for side, has in enumerate((has_low, has_high)):

        @pl.when(jnp.logical_not(has))
        def _():
            halo[:, side] = jnp.zeros(halo.shape[:1] + halo.shape[2:], jnp.float32)
            halo_rows[side] = jnp.zeros(halo_rows.shape[1:], jnp.float32)

    def local(get, buffer, row, piece, transposed):
        xa, pa, xb, pb = [get(quad, row, piece) for quad in range(4)]
        detuning, mech, coupling, cavity, phonon, hopping = [coef(kind, row, piece) for kind in range(6)]
        hops = [
            buffer[quad, row, inner(piece, -1)] + buffer[quad, row, inner(piece, 1)] + buffer[quad, 1 - row, inner(piece)]
            for quad in range(2)
        ]
        if transposed:
            return (
                detuning * pa - cavity * xa - coupling * pb + hops[1],
                -detuning * xa - cavity * pa - hops[0],
                -coupling * pa - mech * pb,
                mech * xb - phonon * pb,
            )
        return (
            -cavity * xa - detuning * pa - hopping * hops[1],
            detuning * xa - cavity * pa - coupling * xb + hopping * hops[0],
            mech * pb,
            -mech * xb - phonon * pb - coupling * xa,
        )

    def value_at(quad, row, piece):
        return values[quad, row, inner(piece)]

    def first_at(quad, row, piece):
        return first[quad, row, at(piece)]

    def first_term(run, source, piece):
        for row in range(rows):
            for quad, value in enumerate(local(value_at, source, row, piece, run == 1)):
                first[quad, row, at(piece)] = value
                if quad < 2:
                    partial[quad, row, at(piece)] = coef(5, row, piece) * value if run else value
        if run == 0 or piece not in early:
            send(functools.partial(message, partial, False, run, 1, piece))

    def first_halo(run, source, piece):
        if run == 0 or piece not in early:
            receive(functools.partial(message, source, True, run, 0, piece))
        for row in range(rows):
            halo_x, halo_p = halo[run, row, 0, at(piece)], halo[run, row, 1, at(piece)]
            hopping = coef(5, row, piece)
            if run:
                new_x, new_p = first_at(0, row, piece) + halo_p, first_at(1, row, piece) - halo_x
            else:
                new_x = first_at(0, row, piece) - hopping * halo_p
                new_p = first_at(1, row, piece) + hopping * halo_x
            first[0, row, at(piece)] = new_x
            first[1, row, at(piece)] = new_p
            second[0, row, inner(piece)] = hopping * new_x if run else new_x
            second[1, row, inner(piece)] = hopping * new_p if run else new_p

    def second_term(run, row, piece):
        found = local(first_at, second, row, piece, run == 1)
        return [value_at(quad, row, piece) + first_at(quad, row, piece) + 0.5 * found[quad] for quad in range(4)]

    def last_halo(run, source, piece):
        if run == 0 or piece not in early:
            receive(functools.partial(message, partial, False, run, 1, piece))
        found = []
        for row in range(rows):
            beyond = coefs[6 * rows + row, at(piece)]
            own_x, own_p = source[0, row, inner(piece)], source[1, row, inner(piece)]
            halo_x, halo_p = halo[run, row, 2, at(piece)], halo[run, row, 3, at(piece)]
            if run:
                add_x, add_p = 0.5 * (halo_p - beyond * own_x), -0.5 * (halo_x + beyond * own_p)
            else:
                hopping = 0.5 * coef(5, row, piece)
                add_x, add_p = -hopping * (halo_p + beyond * own_x), hopping * (halo_x - beyond * own_p)
            found.append((add_x, add_p))
        return found

    pl.semaphore_wait(barrier, jnp.where(me > 0, 1, 0) + jnp.where(me < count - 1, 1, 0) + len(friends))
    send(rates)
    load_z.wait()
    for piece in range(parts):
        send(functools.partial(message, values, True, 0, 0, piece))
    for piece in range(parts):
        first_term(0, values, piece)

    load_noise.wait()
    load_bar.wait()
    for piece in range(parts):
        for quad in range(quads):
            for row in range(rows):
                where = strip(piece, quad, row)
                all_high[where, cols:size], all_low[where, cols:size] = halves(noise_in[quad, row, at(piece)])
                all_high[where, size:], all_low[where, size:] = halves(bar_in[quad, row, at(piece)])

    def accumulate(acc, start, stop, begin, fresh):
        lines = slice(start, stop)
        high = all_high[lines, begin : begin + cols]
        left = jnp.concatenate([high, all_low[lines, begin : begin + cols]], axis=1)
        both = dot16(left, all_high[lines, begin:], (0, 0))
        found = both[:cols] + both[cols:] + dot16(high, all_low[lines, begin:], (0, 0))
        acc[...] = found if fresh else acc[...] + found

    for piece in range(parts):
        accumulate(acc_n, piece * block, (piece + 1) * block, cols, piece == 0)

    receive(rates)
    sides = [halo_rows[0].T, halo_rows[1].T]
    for side in range(2):
        index = 10 - 8 + (rows - 1 if side == 0 else 0)
        coefs[6 * rows + side] = jnp.broadcast_to(sides[side][:, index : index + 1], (cells, cols))

    def finish(piece):
        for row in range(rows):
            found = second_term(0, row, piece)
            for quad in range(2):
                light[quad, row, at(piece)] = found[quad]
            for quad in range(2, 4):
                where = strip(piece, quad, row)
                all_high[where, :cols], all_low[where, :cols] = halves(found[quad])
            if piece in early:
                first[3, row, at(piece)] = found[3]
        accumulate(acc_z, piece * block + block // 2, (piece + 1) * block, 0, piece == 0)

    for piece in range(parts):
        first_halo(0, values, piece)
        if piece:
            finish(piece - 1)
    finish(parts - 1)
    for piece in range(parts):
        for row, added in enumerate(last_halo(0, values, piece)):
            for quad in range(2):
                where = strip(piece, quad, row)
                light[quad, row, at(piece)] = light[quad, row, at(piece)] + added[quad]
                all_high[where, :cols], all_low[where, :cols] = halves(light[quad, row, at(piece)])
        accumulate(acc_z, piece * block, piece * block + block // 2, 0, False)

    def fill_ahead():
        for slot, piece in enumerate(early):
            for row in range(rows):
                for part in range(4):

                    def get(quad, line, shift=0):
                        where = slice(piece * chunk + shift, (piece + 1) * chunk + shift)
                        if part == 0:
                            return first[3, line, where] if quad == 3 else light[quad, line, where]
                        if part == 1:
                            return noise_in[quad, line, where]
                        return bar_in[quad, line, where, (part - 2) * cols : (part - 1) * cols]

                    def hop_rate(shift):
                        return coefs[5 * rows + row, piece * chunk + shift : (piece + 1) * chunk + shift]

                    xa, pa, pb = get(0, row), get(1, row), get(3, row)
                    hops = [
                        hop_rate(-1) * get(quad, row, -1)
                        + hop_rate(1) * get(quad, row, 1)
                        + coef(5, 1 - row, piece) * get(quad, 1 - row)
                        for quad in range(2)
                    ]
                    detuning, coupling, cavity = [coef(kind, row, piece) for kind in (0, 2, 3)]
                    found_x = detuning * pa - cavity * xa - coupling * pb + hops[1]
                    found_p = -detuning * xa - cavity * pa - hops[0]
                    for plane, value in enumerate((xa, pa, found_x, found_p)):
                        ahead_out[row, slot, plane * chunk : (plane + 1) * chunk, part * cols : (part + 1) * cols] = (
                            hop_rate(0) * value
                        )

    gram_part[:cols] = acc_z[:, :cols]
    gram_part[cols:size] = acc_z[:, cols:size]
    gram_part[size : size + cols] = acc_n[:, :cols]
    if gram_part.shape[0] > size + cols:
        gram_part[size + cols :] = jnp.zeros((gram_part.shape[0] - size - cols, cols), jnp.float32)
    gram_steps = reduction(count, *gram_scratch)
    cross_steps = reduction(count, *cross_scratch)
    next(gram_steps)
    for part, (acc, begin) in enumerate(((acc_z, size), (acc_z, size + cols), (acc_n, cols), (acc_n, size))):
        cross_part[part * cols : (part + 1) * cols] = acc[:, begin : begin + cols]
    next(cross_steps)
    next(gram_steps)
    fill_ahead()
    for piece in range(parts):
        sent(functools.partial(message, values, True, 0, 0, piece))
        sent(functools.partial(message, partial, False, 0, 1, piece))
    sent(rates)
    next(gram_steps)
    next(cross_steps)
    next(gram_steps)
    next(cross_steps)
    next(gram_steps, None)
    for slot in range(len(early)):
        send(functools.partial(ahead, slot))

    row_ids = lax.broadcasted_iota(jnp.int32, (size, size), 0)
    col_ids = lax.broadcasted_iota(jnp.int32, (size, size), 1)
    work[:cols, :cols] = gram_full[:cols]
    work[:cols, cols:size] = gram_full[cols:size]
    work[cols:, :cols] = jnp.zeros((cols, cols), jnp.float32)
    work[cols:, cols:size] = gram_full[size : size + cols]
    work[:, size:] = (row_ids == col_ids).astype(jnp.float32)
    for start in range(0, size, tile):
        stop = start + tile
        small = tile_inverse(work[start:stop, start:stop])
        panel = packed_rows(small, work[start:stop, :])
        work[start:stop, :] = panel
        if stop < size:
            base, end = stop // 128 * 128, size + (stop + 127) // 128 * 128
            update = packed(panel[:, base:size], panel[:, base:end])
            work[stop:, base:end] = work[stop:, base:end] - update[stop - base :]
        if start // tile in (4, 7):
            next(cross_steps, None)
    upper = jnp.where(row_ids <= col_ids, work[:, :size], 0.0)
    inverse = jnp.where(row_ids >= col_ids, work[:, size:], 0.0)
    load_rbar.wait()
    bar = jnp.where(row_ids <= col_ids, rbar_ref[...], 0.0)
    cross = jnp.concatenate(
        [
            jnp.concatenate([cross_full[:cols], cross_full[cols:size]], axis=1),
            jnp.concatenate([cross_full[size : size + cols], cross_full[size + cols :]], axis=1),
        ],
        axis=0,
    )
    middle = high_mul(upper, bar, (1, 1)) - high_mul(cross.T, inverse, (1, 1))
    symmetric = jnp.where(row_ids >= col_ids, middle, middle.T)
    mix = high_mul(inverse.T, high_mul(symmetric, inverse, (1, 0)), (1, 0))
    for begin, value in ((0, mix), (size, inverse)):
        lines = slice(begin, begin + size)
        high, rest = halves(value)
        weight_z[lines, :cols], weight_z[lines, cols:] = high[:, :cols], rest[:, :cols]

    def gradient(weight, piece):
        lines = slice(piece * block, (piece + 1) * block)
        both = dot16(all_high[lines], weight[...], (1, 0))
        return both[:, :cols] + both[:, cols:] + dot16(all_low[lines], weight[:, :cols], (1, 0))

    for piece in range(parts):
        grad = gradient(weight_z, piece)
        for quad in range(quads):
            for row in range(rows):
                start = (quad * rows + row) * chunk
                values[quad, row, inner(piece)] = grad[start : start + chunk]
                if quad < 2:
                    hop[quad, row, inner(piece)] = coef(5, row, piece) * grad[start : start + chunk]
        if piece not in early:
            send(functools.partial(message, hop, True, 1, 0, piece))
        if piece:
            first_term(1, hop, piece - 1)
    first_term(1, hop, parts - 1)
    for slot, piece in enumerate(early):
        for side, has in enumerate((has_low, has_high)):

            @pl.when(has)
            def _():
                ahead(slot, side == 0).wait_recv()
                high, rest = halves(ahead_in[side, slot])
                both = dot16(high, weight_z[...], (1, 0))
                edge = both[:, :cols] + both[:, cols:] + dot16(rest, weight_z[:, :cols], (1, 0))
                for plane in range(4):
                    halo[1, side, plane, at(piece)] = edge[plane * chunk : (plane + 1) * chunk]

    for begin, value in ((0, mix), (size, inverse)):
        lines = slice(begin, begin + size)
        weight_n[lines, :cols], weight_n[lines, cols:] = halves(value[:, cols:])
    for piece in range(parts):
        grad = gradient(weight_n, piece)
        for quad in range(quads):
            for row in range(rows):
                start = (quad * rows + row) * chunk
                noise_in[quad, row, at(piece)] = grad[start : start + chunk]
    store_noise = pltpu.make_async_copy(noise_in, noise_out, load_sem.at[1])
    store_noise.start()

    def finish_back(piece):
        for row in range(rows):
            for quad, value in enumerate(second_term(1, row, piece)):
                result[quad, row, at(piece)] = value

    for piece in range(parts):
        first_halo(1, hop, piece)
        if piece:
            finish_back(piece - 1)
    finish_back(parts - 1)
    stores = [store_noise, pltpu.make_async_copy(result.at[2:4], z_out.at[2:4], load_sem.at[0])]
    stores[1].start()
    for piece in range(parts):
        for row, added in enumerate(last_halo(1, hop, piece)):
            for quad in range(2):
                result[quad, row, at(piece)] = result[quad, row, at(piece)] + added[quad]
        stores.append(pltpu.make_async_copy(result.at[0:2, :, at(piece)], z_out.at[0:2, :, at(piece)], load_sem.at[5 + piece]))
        stores[-1].start()
    for store in stores:
        store.wait()
    for slot in range(len(early)):
        sent(functools.partial(ahead, slot))
    for piece in range(parts):
        if piece not in early:
            sent(functools.partial(message, hop, True, 1, 0, piece))
            sent(functools.partial(message, partial, False, 1, 1, piece))


def place_kernel(z_ref, noise_ref, z_out, noise_out, held, load_sem, store_sem):
    quads = z_ref.shape[0]
    loads, stores = [], []
    for index, (source, target) in enumerate(((z_ref, z_out), (noise_ref, noise_out))):
        for quad in range(quads):
            slot = index * quads + quad
            loads.append(pltpu.make_async_copy(source.at[quad], held.at[slot], load_sem.at[slot]))
            stores.append(pltpu.make_async_copy(held.at[slot], target.at[quad], store_sem.at[slot]))
    for load in loads:
        load.start()
    for load, store in zip(loads, stores):
        load.wait()
        store.start()
    for store in stores:
        store.wait()


def place(z_grad, noise_grad):
    far = pl.BlockSpec(memory_space=pl.ANY)
    count = 2 * z_grad.shape[0]
    return pl.pallas_call(
        place_kernel,
        out_shape=tuple(jax.ShapeDtypeStruct(value.shape, value.dtype) for value in (z_grad, noise_grad)),
        in_specs=[far, far],
        out_specs=(far, far),
        scratch_shapes=[
            pltpu.VMEM((count,) + z_grad.shape[1:], jnp.float32),
            pltpu.SemaphoreType.DMA((count,)),
            pltpu.SemaphoreType.DMA((count,)),
        ],
        compiler_params=pltpu.CompilerParams(vmem_limit_bytes=62 * 2**20),
    )(z_grad, noise_grad)


def on_device(cell_coeffs, z_factor, noise_cols, q_bar, r_bar):
    count = lax.axis_size("row")
    quads, rows, cells, cols = z_factor.shape
    size = 2 * cols
    total = quads * rows * cells
    unit = 8 * count
    gram_rows = (size + cols + unit - 1) // unit * unit
    padded = cells + 2 * margin
    plane = (cells, cols)
    far = pl.BlockSpec(memory_space=pl.ANY)

    def floats(*shape):
        return pltpu.VMEM(shape, jnp.float32)

    def shorts(*shape):
        return pltpu.VMEM(shape, jnp.bfloat16)

    z_grad, noise_grad = pl.pallas_call(
        functools.partial(whole_kernel, count),
        out_shape=(
            jax.ShapeDtypeStruct(z_factor.shape, jnp.float32),
            jax.ShapeDtypeStruct(noise_cols.shape, jnp.float32),
        ),
        in_specs=[far] * 5,
        out_specs=(far, far),
        scratch_shapes=[
            floats(*cell_coeffs.shape),
            floats(*r_bar.shape),
            floats(2, len(early), 4 * (cells // parts), 2 * size),
            floats(2, len(early), 4 * (cells // parts), 2 * size),
            floats(16, cells),
            floats(2, 8, cells),
            floats(6 * rows + 2, *plane),
            floats(quads, rows, padded, cols),
            floats(2, rows, padded, cols),
            floats(2, rows, padded, cols),
            floats(quads, rows, *plane),
            floats(2, rows, *plane),
            floats(2, rows, *plane),
            floats(2, 2, 4, *plane),
            floats(quads, rows, *plane),
            floats(quads, rows, cells, size),
            floats(quads, rows, *plane),
            shorts(total, 2 * size),
            shorts(total, 2 * size),
            floats(cols, 2 * size),
            floats(cols, 2 * size - cols),
            floats(size, 2 * size),
            shorts(2 * size, size),
            shorts(2 * size, size),
            pltpu.SemaphoreType.DMA((5 + parts,)),
        ]
        + [pltpu.SemaphoreType.DMA((4 * parts + 1 + len(early),))] * 4
        + reduction_scratch(count, gram_rows, cols)
        + reduction_scratch(count, 4 * cols, cols),
        compiler_params=pltpu.CompilerParams(
            collective_id=0, has_side_effects=True, vmem_limit_bytes=62 * 2**20
        ),
    )(cell_coeffs, z_factor, noise_cols, q_bar, r_bar)
    return place(z_grad, noise_grad)


def solution(mesh):
    return jax.shard_map(
        on_device,
        mesh=mesh,
        in_specs=(
            P(None, "row", None),
            P(None, ("grp", "row"), None, None),
            P(None, ("grp", "row"), None, None),
            P(None, ("grp", "row"), None, None),
            P("grp", None),
        ),
        out_specs=(P(None, ("grp", "row"), None, None), P(None, ("grp", "row"), None, None)),
        check_vma=False,
    )
```
